256 devices in a mesh: sub: 2 (over core), row: 16 (over y, x), col: 8 (over z).
Axes of the slice: x: 4, y: 4, z: 8, core: 2. Of those that a mesh axis runs over, the one named last changes fastest.
Arguments:
- front_entries: float32 [4, 16, 128, 4, 16, 128], P(None, 'row', None, None, ('sub', 'col')), may hold values from -1 to 81, as said below
- child_updates: float32 [2, 3, 16, 128, 6, 8, 128], P('sub', None, 'row', None, None, 'col'), may hold values from -1 to 1, as said below
- row_maps: int32 [2, 48], replicated, may hold values from 0 to 63, as said below
Outputs:
- front_out: float32 [4, 16, 128, 4, 16, 128], P(None, 'row', None, None, ('sub', 'col'))
- factor: float32 [4, 16, 128, 1024], P(None, 'row')
The draws below stay inside these ranges and needn't reach their ends.
Inputs may be any that keep to these rules, and one draw needn't show every extreme that they name: `row_maps`: each child's row is strictly increasing, begins at 0 and ends at 63. `front_entries`: Symmetric; in every draw the assembled front's leading 1024 x 1024 block is positive definite. `child_updates`: each child's update is symmetric.
All inputs are finite; a program needn't handle non-finite values.
Results may differ from the reference program's by a relative error of at most 0.00016.
Values sent between devices are 32-bit elements; how exact they have to be, the bound alone decides.
No kernel may reach another device: no remote copies, remote signals or barrier semaphores. Data moves between devices by JAX's collectives and lax.ppermute only.
A program may use at most 128 MiB of HBM per device.

```python
import jax
import jax.numpy as jnp
from jax import lax

F = 8192
U = 6144
BLK = 128
FB = 64
UB = 48
P_SIZE = 1024
GR = 16
GC = 16
NC = 8
BR = 4
BC = 4
UBR = 3
UBC = 6


def kernel_block(points, reach):
    spread_sum = jnp.zeros((P_SIZE, P_SIZE), jnp.float32)
    for axis_id in range(3):
        coords = points[axis_id]
        spread_sum = spread_sum + jnp.abs(coords[:, None] - coords[None, :])
    return 64.0 * jnp.exp(-spread_sum / reach) + 16.0 * jnp.eye(P_SIZE, dtype=jnp.float32)


def draw_front_entries(key, part):
    key = jax.random.fold_in(key, 11)
    key_vals, key_points = jax.random.split(key)
    uniform_raw = jax.random.uniform(key_vals, (F, F), jnp.float32, -1.0, 1.0)
    point_raw = jax.random.uniform(key_points, (3, P_SIZE), jnp.float32, -1.0, 1.0)
    points = 0.5 + 0.5 * point_raw
    reach = 0.5 * (30.0 / P_SIZE) ** (1.0 / 3.0)
    symmetric = 0.5 * (uniform_raw + uniform_raw.T)
    leading = 0.0035 * symmetric[:P_SIZE, :P_SIZE] + kernel_block(points, reach)
    symmetric = symmetric.at[:P_SIZE, :P_SIZE].set(leading)
    return symmetric.reshape(BR, GR, BLK, BC, GC, BLK)


def draw_child_updates(key, part):
    key = jax.random.fold_in(key, 17)
    uniform_raw = jax.random.uniform(key, (2, U, U), jnp.float32, -1.0, 1.0)
    symmetric = 0.5 * (uniform_raw + jnp.transpose(uniform_raw, (0, 2, 1)))
    child_ids = jnp.arange(U)
    leading = child_ids < P_SIZE
    leading_both = leading[:, None] & leading[None, :]
    symmetric = jnp.where(leading_both[None], 0.002 * symmetric, symmetric)
    return symmetric.reshape(2, UBR, GR, BLK, UBC, NC, BLK)


def draw_row_maps(key, part):
    key = jax.random.fold_in(key, 23)
    result_rows = []
    for k in range(2):
        middle = jax.random.permutation(jax.random.fold_in(key, k), FB - 2) + 1
        chosen = jnp.sort(middle[:UB - 2]).astype(jnp.int32)
        result_rows.append(jnp.concatenate([jnp.zeros((1,), jnp.int32), chosen, jnp.full((1,), FB - 1, jnp.int32)]))
    return jnp.stack(result_rows)


def setup_inputs(seed: int = 0) -> dict:
    streams_of = jax.random.split(jax.random.key(seed), 4)
    return {
        "front_entries": draw_front_entries(jax.random.fold_in(streams_of[3], 71), 0),
        "child_updates": draw_child_updates(jax.random.fold_in(streams_of[3], 71), 0),
        "row_maps": draw_row_maps(jax.random.fold_in(streams_of[3], 71), 0),
    }


def reference(front_entries, child_updates, row_maps):
    entries = front_entries.reshape(F, F)
    summed = jnp.zeros((FB, BLK, FB, BLK), jnp.float32)
    for k in range(2):
        m = row_maps[k].astype(jnp.int32)
        update = child_updates[k].reshape(UB, BLK, UB, BLK)
        summed = summed.at[m[:, None], :, m[None, :], :].add(update.transpose(0, 2, 1, 3))
    front = entries + summed.reshape(F, F)
    diag_factor = jnp.linalg.cholesky(front[:P_SIZE, :P_SIZE])
    solved = jax.scipy.linalg.solve_triangular(diag_factor, front[:, :P_SIZE].T, lower=True).T
    factor = solved.at[:P_SIZE].set(diag_factor)
    lower_part = factor[P_SIZE:]
    trailing = front[P_SIZE:, P_SIZE:] - jnp.dot(lower_part.astype(jnp.float32), lower_part.T.astype(jnp.float32), precision=lax.Precision.HIGHEST, preferred_element_type=jnp.float32)
    front_out = front.at[P_SIZE:, P_SIZE:].set(trailing)
    return (front_out.reshape(BR, GR, BLK, BC, GC, BLK), factor.reshape(BR, GR, BLK, P_SIZE))
```

```python
import functools

import jax
import jax.numpy as jnp
from jax import lax
from jax.experimental import pallas as pl
from jax.experimental.pallas import tpu as pltpu
from jax.sharding import PartitionSpec as P

BLK = 128
FB = 64
UB = 48
P_SIZE = 1024
NPB = 8
GR = 16
NC = 8
CHIPS = GR * NC
F32 = jnp.float32
HIGHEST = lax.Precision.HIGHEST


def dot_full(a, b, dim_a, dim_b):
    return lax.dot_general(
        a, b, (((dim_a,), (dim_b,)), ((), ())), precision=HIGHEST, preferred_element_type=F32
    )


def split(x):
    high = x.astype(jnp.bfloat16)
    return high, (x - high.astype(F32)).astype(jnp.bfloat16)


def dot_split(a, b):
    def dot(x, y):
        return lax.dot_general(x, y, (((1,), (1,)), ((), ())), preferred_element_type=F32)

    return dot(a[0], b[0]) + (dot(a[0], b[1]) + dot(a[1], b[0]))


def row_of(x, t):
    return jnp.broadcast_to(x[t : t + 1, :], x.shape)


def col_of(x, t):
    return jnp.broadcast_to(x[:, t : t + 1], x.shape)


def factor_block(w):
    sub = lax.broadcasted_iota(jnp.int32, (8, BLK), 0)
    lane = lax.broadcasted_iota(jnp.int32, (8, BLK), 1)
    tiles = BLK // 8
    left = [w[8 * i : 8 * i + 8, :] for i in range(tiles)]
    right = [(lane == sub + 8 * i).astype(F32) for i in range(tiles)]
    uppers, inverses = [], []
    for s in range(tiles):
        rows, extra = left[s], right[s]
        diag = [col_of(rows, 8 * s + t) for t in range(8)]
        below = [[col_of(left[i], 8 * s + t) for t in range(8)] for i in range(s + 1, tiles)]
        u, v, pivots = rows, extra, None
        for t in range(0, 8, 2):
            a, b, d = row_of(diag[t], t), row_of(diag[t + 1], t), row_of(diag[t + 1], t + 1)
            ratio = b / a
            inv_det = 1.0 / (a * d - b * b)
            first, cross, second = d * inv_det, b * inv_det, a * inv_det
            at0, at1 = sub == t, sub == t + 1
            r0, r1 = row_of(rows, t), row_of(rows, t + 1)
            e0, e1 = row_of(extra, t), row_of(extra, t + 1)
            u = jnp.where(at0, rows, jnp.where(at1, r1 - ratio * r0, u))
            v = jnp.where(at0, extra, jnp.where(at1, e1 - ratio * e0, v))
            pivots = a if pivots is None else jnp.where(at0, a, pivots)
            pivots = jnp.where(at1, d - b * ratio, pivots)
            c0, c1 = diag[t], diag[t + 1]

            def reduce(x, x0, x1):
                z0 = first * x0 - cross * x1
                z1 = second * x1 - cross * x0
                return jnp.where(at0, z0, jnp.where(at1, z1, x - (c0 * z0 + c1 * z1)))

            rows, extra = reduce(rows, r0, r1), reduce(extra, e0, e1)
            for c in range(t + 2, 8):
                diag[c] = reduce(diag[c], row_of(diag[c], t), row_of(diag[c], t + 1))
        scale = lax.rsqrt(pivots)
        uppers.append(jnp.where(lane >= sub + 8 * s, u * scale, 0.0))
        inverses.append(v * scale)
        row_terms = [row_of(rows, t) for t in range(8)]
        extra_terms = [row_of(extra, t) for t in range(8)]
        for i in range(s + 1, tiles):

            def total(terms):
                parts = [below[i - s - 1][t] * terms[t] for t in range(8)]
                while len(parts) > 1:
                    parts = [parts[2 * n] + parts[2 * n + 1] for n in range(len(parts) // 2)]
                return parts[0]

            left[i] = left[i] - total(row_terms)
            right[i] = right[i] - total(extra_terms)
    return jnp.concatenate(uppers, 0), jnp.concatenate(inverses, 0)


def cholesky_kernel(lead_ref, lower_ref, inverse_ref, panel, upper):
    lower_ref[...] = jnp.zeros_like(lower_ref)

    def step(k, carry):
        for n in range(NPB):

            @pl.when(k == n)
            def _(n=n):
                start = n * BLK
                cols = slice(start, start + BLK)
                for p in range(n, NPB):
                    panel[(p - n) * BLK : (p - n + 1) * BLK, :] = lead_ref[
                        pl.ds(p * NPB + n, BLK, stride=NPB * NPB), :
                    ]
                if n:
                    panel[: P_SIZE - start, :] -= dot_full(
                        lower_ref[start:, :start], lower_ref[cols, :start], 1, 1
                    )

        u, v = factor_block(panel[:BLK, :])
        upper[...] = u
        inverse_ref[k] = v
        for n in range(NPB):

            @pl.when(k == n)
            def _(n=n):
                start = n * BLK
                cols = slice(start, start + BLK)
                lower_ref[cols, cols] = upper[...].T
                if n < NPB - 1:
                    lower_ref[start + BLK :, cols] = dot_full(
                        panel[BLK : P_SIZE - start, :], inverse_ref[n], 1, 1
                    )

        return carry

    lax.fori_loop(0, NPB, step, 0)


def cholesky(lead):
    return pl.pallas_call(
        cholesky_kernel,
        out_shape=[
            jax.ShapeDtypeStruct((P_SIZE, P_SIZE), F32),
            jax.ShapeDtypeStruct((NPB, BLK, BLK), F32),
        ],
        scratch_shapes=[pltpu.VMEM((P_SIZE, BLK), F32), pltpu.VMEM((BLK, BLK), F32)],
        compiler_params=pltpu.CompilerParams(vmem_limit_bytes=40 * 2**20),
        cost_estimate=pl.CostEstimate(
            flops=30_000_000_000, bytes_accessed=9_000_000, transcendentals=0
        ),
        name="cholesky",
    )(lead)


WIDE = 2 * BLK
CHUNK = 256


def solve_kernel(
    where_ref, row_ref, col_ref, lower_ref, inverse_ref, front_ref, factor_ref, out_ref, *scratch
):
    low_hi, low_lo, inv_hi, inv_lo, row_hi, row_lo, col_hi, col_lo = scratch
    grid_row, grid_col = where_ref[0], where_ref[1]
    steps = P_SIZE // WIDE
    low_hi[...], low_lo[...] = split(lower_ref[...])
    for n in range(steps):
        a, b = inverse_ref[2 * n], inverse_ref[2 * n + 1]
        mid = lower_ref[(2 * n + 1) * BLK : (2 * n + 2) * BLK, 2 * n * BLK : (2 * n + 1) * BLK]
        corner = -dot_full(dot_full(b, mid, 1, 0), a, 1, 0)
        whole = jnp.concatenate(
            [
                jnp.concatenate([a, jnp.zeros((BLK, BLK), F32)], 1),
                jnp.concatenate([corner, b], 1),
            ],
            0,
        )
        inv_hi[n], inv_lo[n] = split(whole)

    def solve(strip_ref, hi, lo, keep):
        def chunk(m, carry):
            rows = pl.ds(pl.multiple_of(m * CHUNK, CHUNK), CHUNK)
            for n in range(steps):
                cols = slice(n * WIDE, (n + 1) * WIDE)
                part = strip_ref[rows, cols]
                if n:
                    done = slice(0, n * WIDE)
                    part = part - dot_split(
                        (hi[rows, done], lo[rows, done]), (low_hi[cols, done], low_lo[cols, done])
                    )
                part = dot_split(split(part), (inv_hi[n], inv_lo[n]))
                if keep:
                    factor_ref[rows, cols] = part
                hi[rows, cols], lo[rows, cols] = split(part)
            return carry

        lax.fori_loop(0, strip_ref.shape[0] // CHUNK, chunk, 0)

    solve(row_ref, row_hi, row_lo, True)
    solve(col_ref, col_hi, col_lo, False)

    @pl.when(grid_row < NPB)
    def _():
        rows = pl.ds(pl.multiple_of(jnp.minimum(grid_row, NPB - 1) * BLK, BLK), BLK)
        factor_ref[:BLK, :] = lower_ref[rows, :]

    col_index = lax.broadcasted_iota(jnp.int32, (BLK, out_ref.shape[1]), 1)
    col_on = (col_index >= BLK) | (grid_col >= NPB)
    for b in range(out_ref.shape[0] // BLK):
        rows = slice(b * BLK, (b + 1) * BLK)
        product = dot_split((row_hi[rows, :], row_lo[rows, :]), (col_hi[...], col_lo[...]))
        on = col_on if b else col_on & (grid_row >= NPB)
        out_ref[rows, :] = front_ref[rows, :] - jnp.where(on, product, 0.0)


def solve_and_update(where, row_strip, col_strip, lower, inverses, front):
    n_rows, n_cols = row_strip.shape[0], col_strip.shape[0]
    bf16 = jnp.bfloat16
    whole = pl.BlockSpec(memory_space=pltpu.VMEM)
    return pl.pallas_call(
        solve_kernel,
        in_specs=[pl.BlockSpec(memory_space=pltpu.SMEM)] + [whole] * 5,
        out_specs=[whole, whole],
        out_shape=[
            jax.ShapeDtypeStruct((n_rows, P_SIZE), F32),
            jax.ShapeDtypeStruct((n_rows, n_cols), F32),
        ],
        scratch_shapes=[
            pltpu.VMEM((P_SIZE, P_SIZE), bf16),
            pltpu.VMEM((P_SIZE, P_SIZE), bf16),
            pltpu.VMEM((P_SIZE // WIDE, WIDE, WIDE), bf16),
            pltpu.VMEM((P_SIZE // WIDE, WIDE, WIDE), bf16),
            pltpu.VMEM((n_rows, P_SIZE), bf16),
            pltpu.VMEM((n_rows, P_SIZE), bf16),
            pltpu.VMEM((n_cols, P_SIZE), bf16),
            pltpu.VMEM((n_cols, P_SIZE), bf16),
        ],
        compiler_params=pltpu.CompilerParams(vmem_limit_bytes=48 * 2**20),
        cost_estimate=pl.CostEstimate(
            flops=6_000_000_000, bytes_accessed=14_000_000, transcendentals=0
        ),
        name="solve_and_update",
    )(where, row_strip, col_strip, lower, inverses, front)


def to_chips(x):
    return lax.all_to_all(x, ("row", "col"), 0, 0)


def swap_cores(x):
    return lax.ppermute(x, "sub", [(0, 1), (1, 0)])


def per_device(front_entries, child_updates, row_maps):
    my_row = lax.axis_index("row")
    my_col = lax.axis_index("col")
    my_sub = lax.axis_index("sub")
    entries = front_entries[:, 0, :, :, 0, :]
    update = child_updates[0, :, 0, :, :, 0, :]
    own_map = lax.dynamic_index_in_dim(row_maps, my_sub, 0, keepdims=False)
    other_map = lax.dynamic_index_in_dim(row_maps, 1 - my_sub, 0, keepdims=False)
    blocks = jnp.arange(FB, dtype=jnp.int32)

    entry_panel = entries[:, :, 0, :]
    from_first = swap_cores(entry_panel[2:])
    entry_half = jnp.where(my_sub == 0, entry_panel[:2], from_first)
    panel_out = jnp.concatenate([update[:, :, 0, :], entry_half], 0).transpose(1, 0, 2)
    panel_in = to_chips(panel_out).reshape(GR, NC, 5, BLK)
    child_panel = panel_in[:, :, :3].transpose(2, 0, 1, 3)
    entry_rows = panel_in[:, :, 3:].transpose(2, 0, 1, 3).reshape(FB // 2, NPB, BLK)
    row_pick = (own_map[None, :] == blocks[:, None]).astype(F32)
    col_pick = (own_map[None, :NC] == blocks[:NPB, None]).astype(F32)
    both_pick = (row_pick[:, None, :, None] * col_pick[None, :, None, :]).reshape(
        FB * NPB, UB * NC
    )
    placed = dot_full(both_pick, child_panel.reshape(UB * NC, BLK), 1, 0).reshape(FB, NPB, BLK)
    no_rows = jnp.zeros_like(entry_rows)
    placed = placed + jnp.concatenate(
        [
            jnp.where(my_sub == 0, entry_rows, no_rows),
            jnp.where(my_sub == 0, no_rows, entry_rows),
        ],
        0,
    )
    panel_rows = placed + swap_cores(placed)

    by_grid = panel_rows.reshape(4, 2, NC, NPB, BLK)
    for_cols = lax.dynamic_index_in_dim(by_grid, my_sub, 1, keepdims=False).transpose(1, 0, 2, 3)
    lead_rows = jnp.broadcast_to(panel_rows[None, :NPB], (NC, NPB, NPB, BLK))
    along_col = lax.all_to_all(jnp.concatenate([for_cols, lead_rows], 1), "col", 0, 0)
    lead = lax.all_gather(along_col[:, 4:], "row", axis=0, tiled=True)
    lead = lead.reshape(BLK * NPB * NPB, BLK)
    halves = panel_rows.reshape(2, 2, GR, NPB, BLK)
    for_rows = lax.dynamic_index_in_dim(halves, my_sub, 0, keepdims=False).transpose(1, 0, 2, 3)
    along_row = lax.all_to_all(for_rows, "row", 0, 0)
    row_strip = lax.all_gather(along_row, "col", axis=0)
    col_strip = lax.all_gather(along_col[:, :4], "row", axis=0)

    rest_in = to_chips(update[:, :, 1:, :].transpose(1, 0, 2, 3).reshape(BLK, 15, BLK))
    rest_in = rest_in.reshape(GR, NC, 3, 5, BLK).transpose(2, 0, 3, 1, 4)
    child = jnp.concatenate([child_panel[:, :, None], rest_in], 2).reshape(UB, UB, BLK)
    col_ids = blocks.reshape(4, 2, NC)
    own_cols = lax.dynamic_index_in_dim(col_ids, my_sub, 1, keepdims=False).reshape(-1)
    other_cols = lax.dynamic_index_in_dim(col_ids, 1 - my_sub, 1, keepdims=False).reshape(-1)
    all_cols = jnp.concatenate([own_cols, other_cols])
    widen = (own_map[None, :] == all_cols[:, None]).astype(F32)
    widened = jnp.einsum("qj,ijl->iql", widen, child, precision=HIGHEST)
    arrived = swap_cores(widened[:, FB // 2 :])
    both = jnp.concatenate([widened[:, : FB // 2], arrived], 0).reshape(2 * UB, -1)
    other_pick = (other_map[None, :] == blocks[:, None]).astype(F32)
    summed = dot_full(jnp.concatenate([row_pick, other_pick], 1), both, 1, 0)
    rows_out = summed.reshape(4, GR, 4, NC, BLK).transpose(1, 3, 0, 2, 4).reshape(CHIPS, 16, BLK)
    rows_in = to_chips(rows_out).reshape(BLK, 4, 4, BLK)

    lower, inverses = cholesky(lead)
    front = entries + rows_in.transpose(1, 0, 2, 3)
    other_strip = swap_cores(row_strip)
    first = jnp.where(my_sub == 0, row_strip, other_strip)
    second = jnp.where(my_sub == 0, other_strip, row_strip)
    row_strip = jnp.concatenate([first, second], 2).transpose(2, 1, 0, 3, 4)
    col_strip = col_strip.transpose(2, 0, 1, 3, 4)
    where = jnp.stack([my_row, my_sub * NC + my_col]).astype(jnp.int32)
    factor, updated = solve_and_update(
        where,
        row_strip.reshape(4 * BLK, P_SIZE),
        col_strip.reshape(4 * BLK, P_SIZE),
        lower,
        inverses,
        front.reshape(4 * BLK, 4 * BLK),
    )
    updated = updated.reshape(4, 1, BLK, 4, 1, BLK)
    return updated, factor.reshape(4, 1, BLK, P_SIZE)


def solution(mesh):
    in_specs = (
        P(None, "row", None, None, ("sub", "col"), None),
        P("sub", None, "row", None, None, "col", None),
        P(),
    )
    out_specs = (P(None, "row", None, None, ("sub", "col"), None), P(None, "row", None, None))
    return jax.shard_map(
        per_device, mesh=mesh, in_specs=in_specs, out_specs=out_specs, check_vma=False
    )
```

```python
import functools

import jax
import jax.numpy as jnp
from jax import lax
from jax.experimental import pallas as pl
from jax.experimental.pallas import tpu as pltpu
from jax.sharding import PartitionSpec as P

BLK = 128
FB = 64
UB = 48
P_SIZE = 1024
NPB = 8
GR = 16
NC = 8
CHIPS = GR * NC
F32 = jnp.float32
HIGHEST = lax.Precision.HIGHEST


def dot_full(a, b, dim_a, dim_b):
    return lax.dot_general(
        a, b, (((dim_a,), (dim_b,)), ((), ())), precision=HIGHEST, preferred_element_type=F32
    )


def split(x):
    high = x.astype(jnp.bfloat16)
    return high, (x - high.astype(F32)).astype(jnp.bfloat16)


def dot_split(a, b):
    def dot(x, y):
        return lax.dot_general(x, y, (((1,), (1,)), ((), ())), preferred_element_type=F32)

    return dot(a[0], b[0]) + (dot(a[0], b[1]) + dot(a[1], b[0]))


def row_of(x, t):
    return jnp.broadcast_to(x[t : t + 1, :], x.shape)


def col_of(x, t):
    return jnp.broadcast_to(x[:, t : t + 1], x.shape)


def factor_block(w):
    sub = lax.broadcasted_iota(jnp.int32, (8, BLK), 0)
    lane = lax.broadcasted_iota(jnp.int32, (8, BLK), 1)
    tiles = BLK // 8
    left = [w[8 * i : 8 * i + 8, :] for i in range(tiles)]
    right = [(lane == sub + 8 * i).astype(F32) for i in range(tiles)]
    uppers, inverses = [], []
    for s in range(tiles):
        rows, extra = left[s], right[s]
        diag = [col_of(rows, 8 * s + t) for t in range(8)]
        below = [[col_of(left[i], 8 * s + t) for t in range(8)] for i in range(s + 1, tiles)]
        u, v, pivots = rows, extra, None
        for t in range(0, 8, 2):
            a, b, d = row_of(diag[t], t), row_of(diag[t + 1], t), row_of(diag[t + 1], t + 1)
            ratio = b / a
            inv_det = 1.0 / (a * d - b * b)
            first, cross, second = d * inv_det, b * inv_det, a * inv_det
            at0, at1 = sub == t, sub == t + 1
            r0, r1 = row_of(rows, t), row_of(rows, t + 1)
            e0, e1 = row_of(extra, t), row_of(extra, t + 1)
            u = jnp.where(at0, rows, jnp.where(at1, r1 - ratio * r0, u))
            v = jnp.where(at0, extra, jnp.where(at1, e1 - ratio * e0, v))
            pivots = a if pivots is None else jnp.where(at0, a, pivots)
            pivots = jnp.where(at1, d - b * ratio, pivots)
            c0, c1 = diag[t], diag[t + 1]

            def reduce(x, x0, x1):
                z0 = first * x0 - cross * x1
                z1 = second * x1 - cross * x0
                return jnp.where(at0, z0, jnp.where(at1, z1, x - (c0 * z0 + c1 * z1)))

            rows, extra = reduce(rows, r0, r1), reduce(extra, e0, e1)
            for c in range(t + 2, 8):
                diag[c] = reduce(diag[c], row_of(diag[c], t), row_of(diag[c], t + 1))
        scale = lax.rsqrt(pivots)
        uppers.append(jnp.where(lane >= sub + 8 * s, u * scale, 0.0))
        inverses.append(v * scale)
        row_terms = [row_of(rows, t) for t in range(8)]
        extra_terms = [row_of(extra, t) for t in range(8)]
        for i in range(s + 1, tiles):

            def total(terms):
                parts = [below[i - s - 1][t] * terms[t] for t in range(8)]
                while len(parts) > 1:
                    parts = [parts[2 * n] + parts[2 * n + 1] for n in range(len(parts) // 2)]
                return parts[0]

            left[i] = left[i] - total(row_terms)
            right[i] = right[i] - total(extra_terms)
    return jnp.concatenate(uppers, 0), jnp.concatenate(inverses, 0)


TRIANGLE = [(p, q) for q in range(NPB) for p in range(q, NPB)]
HALF = len(TRIANGLE) // 2


def cholesky_kernel(core_ref, own_ref, other_ref, lower_ref, inverse_ref, panel, upper):
    first_core = core_ref[0] == 0
    lower_ref[...] = jnp.zeros_like(lower_ref)

    def step(k, carry):
        for n in range(NPB):

            @pl.when(k == n)
            def _(n=n):
                start = n * BLK
                cols = slice(start, start + BLK)
                for p in range(n, NPB):
                    spot = TRIANGLE.index((p, n))
                    rows = slice(spot % HALF * 8, spot % HALF * 8 + 8)
                    own = own_ref[:, rows, :].reshape(BLK, BLK)
                    other = other_ref[:, rows, :].reshape(BLK, BLK)
                    is_own = first_core if spot < HALF else jnp.logical_not(first_core)
                    panel[(p - n) * BLK : (p - n + 1) * BLK, :] = jnp.where(is_own, own, other)
                if n:
                    panel[: P_SIZE - start, :] -= dot_full(
                        lower_ref[start:, :start], lower_ref[cols, :start], 1, 1
                    )

        u, v = factor_block(panel[:BLK, :])
        upper[...] = u
        inverse_ref[k] = v
        for n in range(NPB):

            @pl.when(k == n)
            def _(n=n):
                start = n * BLK
                cols = slice(start, start + BLK)
                lower_ref[cols, cols] = upper[...].T
                if n < NPB - 1:
                    lower_ref[start + BLK :, cols] = dot_full(
                        panel[BLK : P_SIZE - start, :], inverse_ref[n], 1, 1
                    )

        return carry

    lax.fori_loop(0, NPB, step, 0)


def cholesky(core, own, other):
    whole = pl.BlockSpec(memory_space=pltpu.VMEM)
    return pl.pallas_call(
        cholesky_kernel,
        in_specs=[pl.BlockSpec(memory_space=pltpu.SMEM), whole, whole],
        out_specs=[whole, whole],
        out_shape=[
            jax.ShapeDtypeStruct((P_SIZE, P_SIZE), F32),
            jax.ShapeDtypeStruct((NPB, BLK, BLK), F32),
        ],
        scratch_shapes=[pltpu.VMEM((P_SIZE, BLK), F32), pltpu.VMEM((BLK, BLK), F32)],
        compiler_params=pltpu.CompilerParams(vmem_limit_bytes=10 * 2**20),
        cost_estimate=pl.CostEstimate(
            flops=30_000_000_000, bytes_accessed=9_000_000, transcendentals=0
        ),
        name="cholesky",
    )(core, own, other)


WIDE = 2 * BLK
CHUNK = 256
STRIP = 4 * BLK


def solve_kernel(
    where_ref,
    own_ref,
    other_ref,
    col_ref,
    lower_ref,
    inverse_ref,
    entry_ref,
    factor_ref,
    out_ref,
    *scratch,
):
    row_hi, row_lo, col_hi, col_lo, low_hi, low_lo, inv_hi, inv_lo, strip = scratch
    first_core, grid_row, grid_col = where_ref[0] == 0, where_ref[1], where_ref[2]
    steps = P_SIZE // WIDE
    low_hi[...], low_lo[...] = split(lower_ref[...])
    for n in range(steps):
        a, b = inverse_ref[2 * n], inverse_ref[2 * n + 1]
        mid = lower_ref[(2 * n + 1) * BLK : (2 * n + 2) * BLK, 2 * n * BLK : (2 * n + 1) * BLK]
        corner = -dot_full(dot_full(b, mid, 1, 0), a, 1, 0)
        whole = jnp.concatenate(
            [
                jnp.concatenate([a, jnp.zeros((BLK, BLK), F32)], 1),
                jnp.concatenate([corner, b], 1),
            ],
            0,
        )
        inv_hi[n], inv_lo[n] = split(whole)

    def solve(hi, lo, keep):
        def chunk(m, carry):
            rows = pl.ds(pl.multiple_of(m * CHUNK, CHUNK), CHUNK)
            for n in range(steps):
                cols = slice(n * WIDE, (n + 1) * WIDE)
                part = strip[rows, cols]
                if n:
                    done = slice(0, n * WIDE)
                    part = part - dot_split(
                        (hi[rows, done], lo[rows, done]), (low_hi[cols, done], low_lo[cols, done])
                    )
                part = dot_split(split(part), (inv_hi[n], inv_lo[n]))
                if keep:
                    factor_ref[rows, cols] = part
                hi[rows, cols], lo[rows, cols] = split(part)
            return carry

        lax.fori_loop(0, STRIP // CHUNK, chunk, 0)

    for b in range(4):
        for q in range(NPB):
            cols = slice(q * BLK, (q + 1) * BLK)
            strip[b * BLK : (b + 1) * BLK, cols] = col_ref[pl.ds(b * NPB + q, BLK, stride=32), :]
    solve(col_hi, col_lo, False)
    for b in range(4):
        is_own = first_core if b < 2 else jnp.logical_not(first_core)
        for q in range(NPB):
            own = own_ref[pl.ds(16 + b % 2 * NPB + q, BLK, stride=32), :]
            other = other_ref[pl.ds(b % 2 * NPB + q, BLK, stride=16), :]
            cols = slice(q * BLK, (q + 1) * BLK)
            strip[b * BLK : (b + 1) * BLK, cols] = jnp.where(is_own, own, other)
    solve(row_hi, row_lo, True)

    @pl.when(grid_row < NPB)
    def _():
        rows = pl.ds(pl.multiple_of(jnp.minimum(grid_row, NPB - 1) * BLK, BLK), BLK)
        factor_ref[:BLK, :] = lower_ref[rows, :]

    for b in range(4):
        rows = slice(b * BLK, (b + 1) * BLK)
        strip[rows, :STRIP] = dot_split(
            (row_hi[rows, :], row_lo[rows, :]), (col_hi[...], col_lo[...])
        )
        for d in range(4):
            sums = own_ref[pl.ds(b * 4 + d, BLK, stride=32), :]
            if b < d:
                sums = sums.T
            elif b == d:
                sums = jnp.where(grid_row >= grid_col, sums, sums.T)
            spot = pl.ds(b * STRIP + d, BLK, stride=4)
            block = entry_ref[spot, :] + sums
            trail = strip[rows, d * BLK : (d + 1) * BLK]
            if b == 0:
                trail = jnp.where(grid_row >= NPB, trail, 0.0)
            if d == 0:
                trail = jnp.where(grid_col >= NPB, trail, 0.0)
            out_ref[spot, :] = block - trail


def solve_and_update(where, own, other, col_strip, lower, inverses, entries):
    bf16 = jnp.bfloat16
    whole = pl.BlockSpec(memory_space=pltpu.VMEM)
    return pl.pallas_call(
        solve_kernel,
        in_specs=[pl.BlockSpec(memory_space=pltpu.SMEM)] + [whole] * 6,
        out_specs=[whole] * 2,
        out_shape=[
            jax.ShapeDtypeStruct((STRIP, P_SIZE), F32),
            jax.ShapeDtypeStruct((4 * STRIP, BLK), F32),
        ],
        scratch_shapes=[pltpu.VMEM((STRIP, P_SIZE), bf16)] * 4
        + [
            pltpu.VMEM((P_SIZE, P_SIZE), bf16),
            pltpu.VMEM((P_SIZE, P_SIZE), bf16),
            pltpu.VMEM((P_SIZE // WIDE, WIDE, WIDE), bf16),
            pltpu.VMEM((P_SIZE // WIDE, WIDE, WIDE), bf16),
            pltpu.VMEM((STRIP, P_SIZE), F32),
        ],
        compiler_params=pltpu.CompilerParams(vmem_limit_bytes=20 * 2**20),
        cost_estimate=pl.CostEstimate(
            flops=8_000_000_000, bytes_accessed=14_000_000, transcendentals=0
        ),
        name="solve_and_update",
    )(where, own, other, col_strip, lower, inverses, entries)


def to_chips(x):
    return lax.all_to_all(x, ("row", "col"), 0, 0)


def after(x, earlier):
    return lax.optimization_barrier((x, earlier))[0]


def swap_cores(x):
    return lax.ppermute(x, "sub", [(0, 1), (1, 0)])


def per_device(front_entries, child_updates, row_maps):
    my_row = lax.axis_index("row")
    my_col = lax.axis_index("col")
    my_sub = lax.axis_index("sub")
    entries = front_entries[:, 0, :, :, 0, :]
    child_own = child_updates[0, :, 0, :, :, 0, :]
    own_map = lax.dynamic_index_in_dim(row_maps, my_sub, 0, keepdims=False)
    other_map = lax.dynamic_index_in_dim(row_maps, 1 - my_sub, 0, keepdims=False)
    blocks = jnp.arange(FB, dtype=jnp.int32)
    where = jnp.stack([my_sub, my_row, my_sub * NC + my_col]).astype(jnp.int32)

    entry_panel = entries[:, :, 0, :]
    from_first = swap_cores(entry_panel[2:])
    entry_half = jnp.where(my_sub == 0, entry_panel[:2], from_first)
    counts = [2 * b + 2 for b in range(3)]
    slices_out = jnp.concatenate(
        [child_own[b, :, :count, :] for b, count in enumerate(counts)]
        + [entry_half.transpose(1, 0, 2)],
        1,
    )
    slices_in = to_chips(slices_out).reshape(GR, NC, 14, BLK)
    lower_child, start = [], 0
    for count in counts:
        part = slices_in[:, :, start : start + count].transpose(0, 2, 1, 3)
        part = jnp.pad(part, ((0, 0), (0, 6 - count), (0, 0), (0, 0)))
        lower_child.append(part.reshape(GR, UB, BLK))
        start += count
    lower_child = jnp.concatenate(lower_child, 0)
    entry_rows = slices_in[:, :, start:].transpose(2, 0, 1, 3).reshape(FB // 2, NPB, BLK)

    row_pick = (own_map[None, :] == blocks[:, None]).astype(F32)
    col_pick = (own_map[None, :NPB] == blocks[:NPB, None]).astype(F32)
    both_pick = (row_pick[:, None, :, None] * col_pick[None, :, None, :]).reshape(
        FB * NPB, UB * NPB
    )
    child_panel = lower_child[:, :NPB].reshape(UB * NPB, BLK)
    placed = dot_full(both_pick, child_panel, 1, 0).reshape(FB, NPB, BLK)
    no_rows = jnp.zeros_like(entry_rows)
    placed = placed + jnp.concatenate(
        [
            jnp.where(my_sub == 0, entry_rows, no_rows),
            jnp.where(my_sub == 0, no_rows, entry_rows),
        ],
        0,
    )
    panel_rows = placed + swap_cores(placed)

    by_grid = panel_rows.reshape(4, 2, NC, NPB, BLK)
    for_cols = lax.dynamic_index_in_dim(by_grid, my_sub, 1, keepdims=False).transpose(1, 0, 2, 3)
    triangle = jnp.concatenate([panel_rows[q:NPB, q] for q in range(NPB)], 0)
    triangle = lax.dynamic_index_in_dim(triangle.reshape(2, HALF, BLK), my_sub, 0, False)
    triangle = jnp.broadcast_to(triangle[None], (NC, HALF, BLK))
    along_col = lax.all_to_all(
        jnp.concatenate([for_cols.reshape(NC, 32, BLK), triangle], 1), "col", 0, 0
    )
    col_strip = lax.all_gather(along_col[:, :32], "row", axis=0)
    ids = jnp.arange(UB, dtype=jnp.int32)
    below = (ids[:, None] > ids[None, :])[:, :, None]
    on_or_below = (ids[:, None] >= ids[None, :])[:, :, None]
    child = jnp.where(on_or_below, lower_child, 0.0)
    child = child + jnp.where(below, lower_child, 0.0).transpose(1, 0, 2)
    col_ids = blocks.reshape(4, 2, NC)
    own_cols = lax.dynamic_index_in_dim(col_ids, my_sub, 1, keepdims=False).reshape(-1)
    other_cols = lax.dynamic_index_in_dim(col_ids, 1 - my_sub, 1, keepdims=False).reshape(-1)
    all_cols = jnp.concatenate([own_cols, other_cols])
    widen = (own_map[None, :] == all_cols[:, None]).astype(F32)
    widened = jnp.einsum("qj,ijl->iql", widen, child, precision=HIGHEST)
    arrived = swap_cores(widened[:, FB // 2 :])
    both = jnp.concatenate([widened[:, : FB // 2], arrived], 0).reshape(2 * UB, -1)
    lead = along_col[:, 32:].transpose(1, 0, 2).reshape(HALF * 8, BLK)
    lead = jnp.broadcast_to(after(lead, both)[None], (GR, HALF * 8, BLK))
    lead = lax.all_to_all(lead, "row", 0, 0)

    other_pick = (other_map[None, :] == blocks[:, None]).astype(F32)
    summed = dot_full(jnp.concatenate([row_pick, other_pick], 1), both, 1, 0)
    sums = summed.reshape(4, GR, 4, NC, BLK).transpose(1, 3, 0, 2, 4).reshape(GR, NC, 16, BLK)
    halves = panel_rows.reshape(2, 2, GR, NPB, BLK)
    for_rows = lax.dynamic_index_in_dim(halves, my_sub, 0, keepdims=False).transpose(1, 0, 2, 3)
    for_rows = jnp.broadcast_to(for_rows.reshape(GR, 1, 16, BLK), (GR, NC, 16, BLK))
    rows_out = jnp.concatenate([sums, for_rows], 2).reshape(CHIPS, 32, BLK)
    rows_in = to_chips(after(rows_out, lead))

    lower, inverses = cholesky(where, lead, swap_cores(lead))
    rows_in = after(rows_in, lower)
    factor, updated = solve_and_update(
        where,
        rows_in.reshape(CHIPS * 32, BLK),
        swap_cores(rows_in[:, 16:]).reshape(CHIPS * 16, BLK),
        col_strip.reshape(CHIPS * 32, BLK),
        lower,
        inverses,
        entries.reshape(4 * STRIP, BLK),
    )
    updated = updated.reshape(4, 1, BLK, 4, 1, BLK)
    return updated, factor.reshape(4, 1, BLK, P_SIZE)


def solution(mesh):
    in_specs = (
        P(None, "row", None, None, ("sub", "col"), None),
        P("sub", None, "row", None, None, "col", None),
        P(),
    )
    out_specs = (P(None, "row", None, None, ("sub", "col"), None), P(None, "row", None, None))
    return jax.shard_map(
        per_device, mesh=mesh, in_specs=in_specs, out_specs=out_specs, check_vma=False
    )
```

```python
import functools

import jax
import jax.numpy as jnp
from jax import lax
from jax.experimental import pallas as pl
from jax.experimental.pallas import tpu as pltpu
from jax.sharding import PartitionSpec as P

BLK = 128
FB = 64
UB = 48
P_SIZE = 1024
NPB = 8
GR = 16
NC = 8
CHIPS = GR * NC
F32 = jnp.float32
HIGHEST = lax.Precision.HIGHEST


def dot_full(a, b, dim_a, dim_b):
    return lax.dot_general(
        a, b, (((dim_a,), (dim_b,)), ((), ())), precision=HIGHEST, preferred_element_type=F32
    )


def split(x):
    high = x.astype(jnp.bfloat16)
    return high, (x - high.astype(F32)).astype(jnp.bfloat16)


def dot_split(a, b):
    left = jnp.concatenate([a[0], a[0], a[1]], 1)
    right = jnp.concatenate([b[0], b[1], b[0]], 1)
    return lax.dot_general(left, right, (((1,), (1,)), ((), ())), preferred_element_type=F32)


def split_rows(x):
    def head(y):
        return y.astype(jnp.bfloat16).astype(F32)

    high = head(x)
    mid = head(x - high)
    return high, mid, head(x - high - mid)


def stacked(parts):
    return jnp.concatenate(parts, 0).astype(jnp.bfloat16)


def reciprocal(x):
    guess = pltpu.reciprocal(x, approx=True)
    return guess * (2.0 - x * guess)


def row_of(x, t):
    return jnp.broadcast_to(x[t : t + 1, :], x.shape)


def col_of(x, t):
    return jnp.broadcast_to(x[:, t : t + 1], x.shape)


def products(columns, rows):
    parts = [c * r for c, r in zip(columns, rows, strict=True)]
    while len(parts) > 1:
        parts = [parts[2 * n] + parts[2 * n + 1] for n in range(len(parts) // 2)]
    return parts[0]


NEAR = 2


def factor_block(w):
    sub = lax.broadcasted_iota(jnp.int32, (8, BLK), 0)
    lane = lax.broadcasted_iota(jnp.int32, (8, BLK), 1)
    tiles = BLK // 8
    left = [w[8 * i : 8 * i + 8, :] for i in range(tiles)]
    right = [(lane == sub + 8 * i).astype(F32) for i in range(tiles)]
    uppers, inverses = [], []
    diag = [col_of(left[0], t) for t in range(8)]
    for s in range(tiles):
        rows, extra = left[s], right[s]
        raw, last = rows, s == tiles - 1
        ahead, later, near = [], [], {}
        if not last:
            ahead = [col_of(rows, 8 * s + 8 + t) for t in range(8)]
            later = [col_of(left[s + 1], 8 * s + 8 + t) for t in range(8)]
            near = {
                i: [col_of(left[i], 8 * s + t) for t in range(8)]
                for i in range(s + 1, min(tiles, s + 1 + NEAR))
            }
        u, v, pivots = rows, extra, None
        for t in range(0, 8, 2):
            c0, c1 = diag[t], diag[t + 1]
            a, b, d = row_of(c0, t), row_of(c1, t), row_of(c1, t + 1)
            inv_det = reciprocal(a * d - b * b)
            at0, at1 = sub == t, sub == t + 1
            either = at0 | at1
            g0 = jnp.where(at0, -d, jnp.where(at1, b, c0 * d - c1 * b))
            g1 = jnp.where(at0, b, jnp.where(at1, -a, c1 * a - c0 * b))
            h0, h1 = g0 * inv_det, g1 * inv_det
            ratio = b * reciprocal(a)
            u = jnp.where(at0, rows, jnp.where(at1, row_of(rows, t + 1) - ratio * row_of(rows, t), u))
            v = jnp.where(
                at0, extra, jnp.where(at1, row_of(extra, t + 1) - ratio * row_of(extra, t), v)
            )
            pivots = a if pivots is None else jnp.where(at0, a, pivots)
            pivots = jnp.where(at1, d - b * ratio, pivots)

            def reduce(x, soon=False):
                x0, x1, base = row_of(x, t), row_of(x, t + 1), jnp.where(either, 0.0, x)
                if soon:
                    return base - (g0 * x0 + g1 * x1) * inv_det
                return base - (h0 * x0 + h1 * x1)

            for c in range(t + 2, 8):
                diag[c] = reduce(diag[c], c < t + 4)
            ahead = [reduce(x) for x in ahead]
            rows, extra = reduce(rows), reduce(extra)
        scale = lax.rsqrt(pivots)
        uppers.append(jnp.where(lane >= sub + 8 * s, u * scale, 0.0))
        inverses.append(v * scale)
        if last:
            break
        diag = [
            later[c] - products(near[s + 1], [row_of(ahead[c], t) for t in range(8)])
            for c in range(8)
        ]
        row_terms = [row_of(rows, t) for t in range(8)]
        extra_terms = [row_of(extra, t) for t in range(8)]
        for i, columns in near.items():
            left[i] = left[i] - products(columns, row_terms)
            right[i] = right[i] - products(columns, extra_terms)
        if s + 1 + NEAR < tiles:
            high, mid, low = split_rows(raw)
            far_columns = stacked([high, high, mid, mid, high, low])
            high, mid, low = split_rows(jnp.concatenate([rows, extra], 1))
            far_rows = stacked([high, mid, high, mid, low, high])
            far = lax.dot_general(
                far_columns, far_rows, (((0,), (0,)), ((), ())), preferred_element_type=F32
            )
            for i in range(s + 1 + NEAR, tiles):
                left[i] = left[i] - far[8 * i : 8 * i + 8, :BLK]
                right[i] = right[i] - far[8 * i : 8 * i + 8, BLK:]
    return jnp.concatenate(uppers, 0), jnp.concatenate(inverses, 0)


WIDE = 2 * BLK
CHUNK = 512
STRIP = 4 * BLK
STEPS = P_SIZE // WIDE
TRIANGLE = [(p, q) for q in range(NPB) for p in range(q, NPB)]
HALF = len(TRIANGLE) // 2


def cholesky_kernel(
    where_ref,
    own_ref,
    other_ref,
    low_hi,
    low_lo,
    inv_hi,
    inv_lo,
    top_ref,
    lower_ref,
    inverse_ref,
    panel,
    upper,
):
    first_core, grid_row = where_ref[0] == 0, where_ref[1]
    lower_ref[...] = jnp.zeros_like(lower_ref)

    def step(k, carry):
        for n in range(NPB):

            @pl.when(k == n)
            def _(n=n):
                start = n * BLK
                cols = slice(start, start + BLK)
                for p in range(n, NPB):
                    spot = TRIANGLE.index((p, n))
                    rows = slice(spot % HALF * 8, spot % HALF * 8 + 8)
                    own = own_ref[:, rows, :].reshape(BLK, BLK)
                    other = other_ref[:, rows, :].reshape(BLK, BLK)
                    is_own = first_core if spot < HALF else jnp.logical_not(first_core)
                    panel[(p - n) * BLK : (p - n + 1) * BLK, :] = jnp.where(is_own, own, other)
                if n:
                    panel[: P_SIZE - start, :] -= dot_full(
                        lower_ref[start:, :start], lower_ref[cols, :start], 1, 1
                    )

        u, v = factor_block(panel[:BLK, :])
        upper[...] = u
        inverse_ref[k] = v
        for n in range(NPB):

            @pl.when(k == n)
            def _(n=n):
                start = n * BLK
                cols = slice(start, start + BLK)
                lower_ref[cols, cols] = upper[...].T
                if n < NPB - 1:
                    lower_ref[start + BLK :, cols] = dot_full(
                        panel[BLK : P_SIZE - start, :], inverse_ref[n], 1, 1
                    )

        return carry

    lax.fori_loop(0, NPB, step, 0)
    top_ref[...] = lower_ref[
        pl.ds(pl.multiple_of(jnp.minimum(grid_row, NPB - 1) * BLK, BLK), BLK), :
    ]
    low_hi[...], low_lo[...] = split(lower_ref[...])
    for n in range(STEPS):
        a, b = inverse_ref[2 * n], inverse_ref[2 * n + 1]
        mid = lower_ref[(2 * n + 1) * BLK : (2 * n + 2) * BLK, 2 * n * BLK : (2 * n + 1) * BLK]
        corner = -dot_full(dot_full(b, mid, 1, 0), a, 1, 0)
        whole = jnp.concatenate(
            [
                jnp.concatenate([a, jnp.zeros((BLK, BLK), F32)], 1),
                jnp.concatenate([corner, b], 1),
            ],
            0,
        )
        inv_hi[n], inv_lo[n] = split(whole)


def cholesky(where, own, other):
    bf16 = jnp.bfloat16
    whole = pl.BlockSpec(memory_space=pltpu.VMEM)
    return pl.pallas_call(
        cholesky_kernel,
        in_specs=[pl.BlockSpec(memory_space=pltpu.SMEM), whole, whole],
        out_specs=[whole] * 5,
        out_shape=[jax.ShapeDtypeStruct((P_SIZE, P_SIZE), bf16)] * 2
        + [jax.ShapeDtypeStruct((STEPS, WIDE, WIDE), bf16)] * 2
        + [jax.ShapeDtypeStruct((BLK, P_SIZE), F32)],
        scratch_shapes=[
            pltpu.VMEM((P_SIZE, P_SIZE), F32),
            pltpu.VMEM((NPB, BLK, BLK), F32),
            pltpu.VMEM((P_SIZE, BLK), F32),
            pltpu.VMEM((BLK, BLK), F32),
        ],
        compiler_params=pltpu.CompilerParams(vmem_limit_bytes=60 * 2**20),
        cost_estimate=pl.CostEstimate(
            flops=1, bytes_accessed=1, transcendentals=0
        ),
        name="cholesky",
    )(where, own, other)


def solve_strip(strip, lower, inverse, keep):
    for m in range(STRIP // CHUNK):
        rows = slice(m * CHUNK, (m + 1) * CHUNK)
        high, low = [], []
        for n in range(STEPS):
            cols = slice(n * WIDE, (n + 1) * WIDE)
            part = strip[rows, cols]
            if n:
                done = slice(0, n * WIDE)
                part = part - dot_split(
                    (jnp.concatenate(high, 1), jnp.concatenate(low, 1)),
                    (lower[0][cols, done], lower[1][cols, done]),
                )
            part = dot_split(split(part), (inverse[0][n], inverse[1][n]))
            hi, lo = split(part)
            high.append(hi)
            low.append(lo)
            keep(rows, cols, part, hi, lo)


def column_kernel(
    col_hbm,
    low_hi_hbm,
    low_lo_hbm,
    inv_hi_hbm,
    inv_lo_hbm,
    col_hi,
    col_lo,
    col_ref,
    low_hi,
    low_lo,
    inv_hi,
    inv_lo,
    strip,
    sems,
):
    pairs = [
        (col_hbm, col_ref),
        (inv_hi_hbm, inv_hi),
        (inv_lo_hbm, inv_lo),
        (low_hi_hbm, low_hi),
        (low_lo_hbm, low_lo),
    ]
    loads = [pltpu.make_async_copy(a, b, sems.at[n]) for n, (a, b) in enumerate(pairs)]
    for load in loads:
        load.start()
    loads[0].wait()
    for b in range(4):
        part = jnp.swapaxes(col_ref[:, b * NPB : (b + 1) * NPB, :], 0, 1)
        for q in range(NPB):
            cols = slice(q * BLK, (q + 1) * BLK)
            strip[b * BLK : (b + 1) * BLK, cols] = part[q]
    for load in loads[1:]:
        load.wait()

    def keep(rows, cols, x, hi, lo):
        col_hi[rows, cols], col_lo[rows, cols] = hi, lo

    solve_strip(strip, (low_hi, low_lo), (inv_hi, inv_lo), keep)


def solve_columns(col_strip, *factor_parts):
    inputs = (col_strip, *factor_parts)
    anywhere = pl.BlockSpec(memory_space=pl.ANY)
    return pl.pallas_call(
        column_kernel,
        in_specs=[anywhere] * len(inputs),
        out_specs=[pl.BlockSpec(memory_space=pltpu.VMEM)] * 2,
        out_shape=[jax.ShapeDtypeStruct((STRIP, P_SIZE), jnp.bfloat16)] * 2,
        scratch_shapes=[pltpu.VMEM(x.shape, x.dtype) for x in inputs]
        + [pltpu.VMEM((STRIP, P_SIZE), F32), pltpu.SemaphoreType.DMA((len(inputs),))],
        compiler_params=pltpu.CompilerParams(vmem_limit_bytes=60 * 2**20),
        cost_estimate=pl.CostEstimate(
            flops=200_000_000_000, bytes_accessed=9_000_000, transcendentals=0
        ),
        name="solve_columns",
    )(*inputs)


def solve_kernel(
    where_ref,
    top_hbm,
    own_hbm,
    other_hbm,
    entry_hbm,
    col_hi_hbm,
    col_lo_hbm,
    low_hi_hbm,
    low_lo_hbm,
    inv_hi_hbm,
    inv_lo_hbm,
    factor_hbm,
    out_hbm,
    top_ref,
    own_ref,
    other_ref,
    entry_ref,
    col_hi,
    col_lo,
    low_hi,
    low_lo,
    inv_hi,
    inv_lo,
    factor_ref,
    out_ref,
    strip,
    row_hi,
    row_lo,
    sems,
):
    first_core, grid_row, grid_col = where_ref[0] == 0, where_ref[1], where_ref[2]
    pairs = [
        (own_hbm, own_ref),
        (other_hbm, other_ref),
        (inv_hi_hbm, inv_hi),
        (inv_lo_hbm, inv_lo),
        (low_hi_hbm, low_hi),
        (low_lo_hbm, low_lo),
        (col_hi_hbm, col_hi),
        (col_lo_hbm, col_lo),
        (top_hbm, top_ref),
        (entry_hbm, entry_ref),
    ]
    loads = [pltpu.make_async_copy(a, b, sems.at[n]) for n, (a, b) in enumerate(pairs)]
    for load in loads:
        load.start()
    for load in loads[:2]:
        load.wait()
    for b in range(4):
        is_own = first_core if b < 2 else jnp.logical_not(first_core)
        half = b % 2 * NPB
        own, other = own_ref[:, 16 + half : 24 + half, :], other_ref[:, half : half + NPB, :]
        picked = jnp.swapaxes(jnp.where(is_own, own, other), 0, 1)
        for q in range(NPB):
            strip[b * BLK : (b + 1) * BLK, q * BLK : (q + 1) * BLK] = picked[q]
    for load in loads[2:6]:
        load.wait()

    def keep_row(rows, cols, x, hi, lo):
        factor_ref[rows, cols] = x
        row_hi[rows, cols], row_lo[rows, cols] = hi, lo

    solve_strip(strip, (low_hi, low_lo), (inv_hi, inv_lo), keep_row)
    for load in loads[6:]:
        load.wait()

    @pl.when(grid_row < NPB)
    def _():
        factor_ref[:BLK, :] = top_ref[...]

    factor_store = pltpu.make_async_copy(factor_ref, factor_hbm, sems.at[10])
    factor_store.start()
    for b in range(4):
        rows = slice(b * BLK, (b + 1) * BLK)
        strip[rows, :STRIP] = dot_split(
            (row_hi[rows, :], row_lo[rows, :]), (col_hi[...], col_lo[...])
        )
        if b % 2 == 0:
            all_sums = jnp.swapaxes(own_ref[:, b * 4 : b * 4 + 8, :], 0, 1)
        for d in range(4):
            sums = all_sums[b % 2 * 4 + d]
            if b < d:
                sums = sums.T
            elif b == d:
                sums = jnp.where(grid_row >= grid_col, sums, sums.T)
            spot = pl.ds(b * STRIP + d, BLK, stride=4)
            block = entry_ref[spot, :] + sums
            trail = strip[rows, d * BLK : (d + 1) * BLK]
            if b == 0:
                trail = jnp.where(grid_row >= NPB, trail, 0.0)
            if d == 0:
                trail = jnp.where(grid_col >= NPB, trail, 0.0)
            out_ref[spot, :] = block - trail
    out_store = pltpu.make_async_copy(out_ref, out_hbm, sems.at[11])
    out_store.start()
    factor_store.wait()
    out_store.wait()


def solve_and_update(where, top, own, other, entries, *solved):
    bf16 = jnp.bfloat16
    inputs = (top, own, other, entries, *solved)
    outputs = [
        jax.ShapeDtypeStruct((STRIP, P_SIZE), F32),
        jax.ShapeDtypeStruct((4 * STRIP, BLK), F32),
    ]
    anywhere = pl.BlockSpec(memory_space=pl.ANY)
    return pl.pallas_call(
        solve_kernel,
        in_specs=[pl.BlockSpec(memory_space=pltpu.SMEM)] + [anywhere] * len(inputs),
        out_specs=[anywhere] * 2,
        out_shape=outputs,
        scratch_shapes=[pltpu.VMEM(x.shape, x.dtype) for x in (*inputs, *outputs)]
        + [pltpu.VMEM((STRIP, P_SIZE), F32)]
        + [pltpu.VMEM((STRIP, P_SIZE), bf16)] * 2
        + [pltpu.SemaphoreType.DMA((12,))],
        compiler_params=pltpu.CompilerParams(vmem_limit_bytes=60 * 2**20),
        cost_estimate=pl.CostEstimate(
            flops=6_000_000_000, bytes_accessed=14_000_000, transcendentals=0
        ),
        name="solve_and_update",
    )(where, *inputs)


def pack_kernel(inverse_map_ref, own_ref, other_ref, panel_ref, out_ref):
    for p in range(FB):
        b, r = divmod(p, GR)
        total = jnp.zeros((4 * NC, BLK), F32)
        for k, child in enumerate((own_ref, other_ref)):
            spot = inverse_map_ref[k, p]
            total = total + jnp.where(spot >= 0, child[jnp.maximum(spot, 0)], 0.0)
        for d in range(4):
            out_ref[pl.ds(r * 256 + b * 4 + d, NC, stride=32), :] = total[d * NC : (d + 1) * NC]
    for h in range(2):
        for r in range(GR):
            rows = panel_ref[h, r]
            for c in range(NC):
                out_ref[pl.ds(r * 256 + c * 32 + 16 + h * 8, NPB), :] = rows


def pack(inverse_maps, own, other, panel):
    whole = pl.BlockSpec(memory_space=pltpu.VMEM)
    return pl.pallas_call(
        pack_kernel,
        in_specs=[pl.BlockSpec(memory_space=pltpu.SMEM)] + [whole] * 3,
        out_specs=whole,
        out_shape=jax.ShapeDtypeStruct((CHIPS * 32, BLK), F32),
        compiler_params=pltpu.CompilerParams(vmem_limit_bytes=12 * 2**20),
        cost_estimate=pl.CostEstimate(flops=0, bytes_accessed=8_000_000, transcendentals=0),
        name="pack",
    )(inverse_maps, own, other, panel)


def to_chips(x):
    return lax.all_to_all(x, ("row", "col"), 0, 0)


def after(x, earlier):
    return lax.optimization_barrier((x, earlier))[0]


def swap_cores(x):
    return lax.ppermute(x, "sub", [(0, 1), (1, 0)])


def per_device(front_entries, child_updates, row_maps):
    my_row = lax.axis_index("row")
    my_col = lax.axis_index("col")
    my_sub = lax.axis_index("sub")
    entries = front_entries[:, 0, :, :, 0, :]
    child_own = child_updates[0, :, 0, :, :, 0, :]
    own_map = lax.dynamic_index_in_dim(row_maps, my_sub, 0, keepdims=False)
    other_map = lax.dynamic_index_in_dim(row_maps, 1 - my_sub, 0, keepdims=False)
    blocks = jnp.arange(FB, dtype=jnp.int32)
    where = jnp.stack([my_sub, my_row, my_sub * NC + my_col]).astype(jnp.int32)

    entry_panel = entries[:, :, 0, :]
    from_first = swap_cores(entry_panel[2:])
    entry_half = jnp.where(my_sub == 0, entry_panel[:2], from_first)
    counts = [2 * b + 2 for b in range(3)]
    slices_out = jnp.concatenate(
        [child_own[b, :, :count, :] for b, count in enumerate(counts)]
        + [entry_half.transpose(1, 0, 2)],
        1,
    )
    slices_in = to_chips(slices_out).reshape(GR, NC, 14, BLK)
    lower_child, start = [], 0
    for count in counts:
        part = slices_in[:, :, start : start + count].transpose(0, 2, 1, 3)
        part = jnp.pad(part, ((0, 0), (0, 6 - count), (0, 0), (0, 0)))
        lower_child.append(part.reshape(GR, UB, BLK))
        start += count
    lower_child = jnp.concatenate(lower_child, 0)
    entry_rows = slices_in[:, :, start:].transpose(2, 0, 1, 3).reshape(FB // 2, NPB, BLK)

    row_pick = (own_map[None, :] == blocks[:, None]).astype(F32)
    col_pick = (own_map[None, :NPB] == blocks[:NPB, None]).astype(F32)
    both_pick = (row_pick[:, None, :, None] * col_pick[None, :, None, :]).reshape(
        FB * NPB, UB * NPB
    )
    child_panel = lower_child[:, :NPB].reshape(UB * NPB, BLK)
    placed = dot_full(both_pick, child_panel, 1, 0).reshape(FB, NPB, BLK)
    no_rows = jnp.zeros_like(entry_rows)
    placed = placed + jnp.concatenate(
        [
            jnp.where(my_sub == 0, entry_rows, no_rows),
            jnp.where(my_sub == 0, no_rows, entry_rows),
        ],
        0,
    )
    panel_rows = placed + swap_cores(placed)

    by_grid = panel_rows.reshape(4, 2, NC, NPB, BLK)
    for_cols = lax.dynamic_index_in_dim(by_grid, my_sub, 1, keepdims=False).transpose(1, 0, 2, 3)
    triangle = jnp.concatenate([panel_rows[q:NPB, q] for q in range(NPB)], 0)
    triangle = lax.dynamic_index_in_dim(triangle.reshape(2, HALF, BLK), my_sub, 0, False)
    triangle = jnp.broadcast_to(triangle[None], (NC, HALF, BLK))
    along_col = lax.all_to_all(
        jnp.concatenate([for_cols.reshape(NC, 32, BLK), triangle], 1), "col", 0, 0
    )
    col_part = along_col[:, :32]
    col_strip = lax.all_gather(col_part, "row", axis=0)
    lead = along_col[:, 32:].transpose(1, 0, 2).reshape(HALF * 8, BLK)
    lead = after(lead, col_part)
    lead = lax.all_to_all(jnp.broadcast_to(lead[None], (GR, HALF * 8, BLK)), "row", 0, 0)

    ids = jnp.arange(UB, dtype=jnp.int32)
    below = (ids[:, None] > ids[None, :])[:, :, None]
    on_or_below = (ids[:, None] >= ids[None, :])[:, :, None]
    lower_child = after(lower_child, along_col)
    child = jnp.where(on_or_below, lower_child, 0.0)
    child = child + jnp.where(below, lower_child, 0.0).transpose(1, 0, 2)
    col_ids = blocks.reshape(4, 2, NC)
    own_cols = lax.dynamic_index_in_dim(col_ids, my_sub, 1, keepdims=False).reshape(-1)
    other_cols = lax.dynamic_index_in_dim(col_ids, 1 - my_sub, 1, keepdims=False).reshape(-1)
    all_cols = jnp.concatenate([own_cols, other_cols])
    widen = (own_map[None, :] == all_cols[:, None]).astype(F32)
    widened = jnp.einsum("qj,ijl->iql", widen, child, precision=HIGHEST)
    kept, arrived = widened[:, : FB // 2], swap_cores(widened[:, FB // 2 :])

    both_maps = jnp.stack([own_map, other_map])
    hit = both_maps[:, None, :] == blocks[None, :, None]
    inverse_maps = jnp.max(jnp.where(hit, ids, -1), axis=2)
    halves = panel_rows.reshape(2, 2, GR, NPB, BLK)
    for_rows = lax.dynamic_index_in_dim(halves, my_sub, 0, keepdims=False)
    rows_out = pack(inverse_maps, kept, arrived, for_rows).reshape(CHIPS, 32, BLK)
    lead, rows_out = lax.optimization_barrier((lead, rows_out))
    other_lead = swap_cores(lead)
    rows_in = to_chips(after(rows_out, other_lead))

    *factor_parts, top = cholesky(where, lead, other_lead)
    columns = solve_columns(col_strip.reshape(CHIPS, 32, BLK), *factor_parts)
    rows_in = after(rows_in, columns[0])
    factor, updated = solve_and_update(
        where,
        top,
        rows_in,
        swap_cores(rows_in[:, 16:]),
        entries.reshape(4 * STRIP, BLK),
        *columns,
        *factor_parts,
    )
    updated = updated.reshape(4, 1, BLK, 4, 1, BLK)
    return updated, factor.reshape(4, 1, BLK, P_SIZE)


def solution(mesh):
    in_specs = (
        P(None, "row", None, None, ("sub", "col"), None),
        P("sub", None, "row", None, None, "col", None),
        P(),
    )
    out_specs = (P(None, "row", None, None, ("sub", "col"), None), P(None, "row", None, None))
    return jax.shard_map(
        per_device, mesh=mesh, in_specs=in_specs, out_specs=out_specs, check_vma=False
    )
```

```python
import functools

import jax
import jax.numpy as jnp
from jax import lax
from jax.experimental import pallas as pl
from jax.experimental.pallas import tpu as pltpu
from jax.sharding import PartitionSpec as P

BLK = 128
FB = 64
UB = 48
P_SIZE = 1024
NPB = 8
GR = 16
NC = 8
CHIPS = GR * NC
F32 = jnp.float32
HIGHEST = lax.Precision.HIGHEST


def dot_full(a, b, dim_a, dim_b):
    return lax.dot_general(
        a, b, (((dim_a,), (dim_b,)), ((), ())), precision=HIGHEST, preferred_element_type=F32
    )


def split(x):
    high = x.astype(jnp.bfloat16)
    return high, (x - high.astype(F32)).astype(jnp.bfloat16)


def dot_split(a, b):
    def dot(x, y):
        return lax.dot_general(x, y, (((1,), (1,)), ((), ())), preferred_element_type=F32)

    return dot(a[0], b[0]) + (dot(a[0], b[1]) + dot(a[1], b[0]))


def split_rows(x):
    def head(y):
        return y.astype(jnp.bfloat16).astype(F32)

    high = head(x)
    mid = head(x - high)
    return high, mid, head(x - high - mid)


def stacked(parts):
    return jnp.concatenate(parts, 0).astype(jnp.bfloat16)


def reciprocal(x):
    guess = pltpu.reciprocal(x, approx=True)
    return guess * (2.0 - x * guess)


def row_of(x, t):
    return jnp.broadcast_to(x[t : t + 1, :], x.shape)


def col_of(x, t):
    return jnp.broadcast_to(x[:, t : t + 1], x.shape)


def products(columns, rows):
    parts = [c * r for c, r in zip(columns, rows, strict=True)]
    while len(parts) > 1:
        parts = [parts[2 * n] + parts[2 * n + 1] for n in range(len(parts) // 2)]
    return parts[0]


NEAR = 2


def factor_block(w):
    sub = lax.broadcasted_iota(jnp.int32, (8, BLK), 0)
    lane = lax.broadcasted_iota(jnp.int32, (8, BLK), 1)
    tiles = BLK // 8
    left = [w[8 * i : 8 * i + 8, :] for i in range(tiles)]
    right = [(lane == sub + 8 * i).astype(F32) for i in range(tiles)]
    uppers, inverses = [], []
    diag = [col_of(left[0], t) for t in range(8)]
    for s in range(tiles):
        rows, extra = left[s], right[s]
        raw, last = rows, s == tiles - 1
        ahead, later, near = [], [], {}
        if not last:
            ahead = [col_of(rows, 8 * s + 8 + t) for t in range(8)]
            later = [col_of(left[s + 1], 8 * s + 8 + t) for t in range(8)]
            near = {
                i: [col_of(left[i], 8 * s + t) for t in range(8)]
                for i in range(s + 1, min(tiles, s + 1 + NEAR))
            }
        u, v, pivots = rows, extra, None
        for t in range(0, 8, 2):
            c0, c1 = diag[t], diag[t + 1]
            a, b, d = row_of(c0, t), row_of(c1, t), row_of(c1, t + 1)
            inv_det = reciprocal(a * d - b * b)
            at0, at1 = sub == t, sub == t + 1
            either = at0 | at1
            g0 = jnp.where(at0, -d, jnp.where(at1, b, c0 * d - c1 * b))
            g1 = jnp.where(at0, b, jnp.where(at1, -a, c1 * a - c0 * b))
            h0, h1 = g0 * inv_det, g1 * inv_det
            ratio = b * reciprocal(a)
            u = jnp.where(at0, rows, jnp.where(at1, row_of(rows, t + 1) - ratio * row_of(rows, t), u))
            v = jnp.where(
                at0, extra, jnp.where(at1, row_of(extra, t + 1) - ratio * row_of(extra, t), v)
            )
            pivots = a if pivots is None else jnp.where(at0, a, pivots)
            pivots = jnp.where(at1, d - b * ratio, pivots)

            def reduce(x, soon=False):
                x0, x1, base = row_of(x, t), row_of(x, t + 1), jnp.where(either, 0.0, x)
                if soon:
                    return base - (g0 * x0 + g1 * x1) * inv_det
                return base - (h0 * x0 + h1 * x1)

            for c in range(t + 2, 8):
                diag[c] = reduce(diag[c], c < t + 4)
            ahead = [reduce(x) for x in ahead]
            rows, extra = reduce(rows), reduce(extra)
        scale = lax.rsqrt(pivots)
        uppers.append(jnp.where(lane >= sub + 8 * s, u * scale, 0.0))
        inverses.append(v * scale)
        if last:
            break
        diag = [
            later[c] - products(near[s + 1], [row_of(ahead[c], t) for t in range(8)])
            for c in range(8)
        ]
        row_terms = [row_of(rows, t) for t in range(8)]
        extra_terms = [row_of(extra, t) for t in range(8)]
        for i, columns in near.items():
            left[i] = left[i] - products(columns, row_terms)
            right[i] = right[i] - products(columns, extra_terms)
        if s + 1 + NEAR < tiles:
            high, mid, low = split_rows(raw)
            far_columns = stacked([high, high, mid, mid, high, low])
            high, mid, low = split_rows(jnp.concatenate([rows, extra], 1))
            far_rows = stacked([high, mid, high, mid, low, high])
            far = lax.dot_general(
                far_columns, far_rows, (((0,), (0,)), ((), ())), preferred_element_type=F32
            )
            for i in range(s + 1 + NEAR, tiles):
                left[i] = left[i] - far[8 * i : 8 * i + 8, :BLK]
                right[i] = right[i] - far[8 * i : 8 * i + 8, BLK:]
    return jnp.concatenate(uppers, 0), jnp.concatenate(inverses, 0)


WIDE = 2 * BLK
STRIP = 4 * BLK
STEPS = P_SIZE // WIDE
TRIANGLE = [(p, q) for q in range(NPB) for p in range(q, NPB)]
HALF = len(TRIANGLE) // 2


def cholesky_kernel(
    where_ref,
    own_ref,
    other_ref,
    low_hi,
    low_lo,
    inv_hi,
    inv_lo,
    top_ref,
    lower_ref,
    inverse_ref,
    panel,
    upper,
):
    first_core, grid_row = where_ref[0] == 0, where_ref[1]
    lower_ref[...] = jnp.zeros_like(lower_ref)

    def step(k, carry):
        for n in range(NPB):

            @pl.when(k == n)
            def _(n=n):
                start = n * BLK
                cols = slice(start, start + BLK)
                for p in range(n, NPB):
                    spot = TRIANGLE.index((p, n))
                    rows = slice(spot % HALF * 8, spot % HALF * 8 + 8)
                    own, other = own_ref[:, rows, :], other_ref[:, rows, :]
                    is_own = first_core if spot < HALF else jnp.logical_not(first_core)
                    block = jnp.swapaxes(jnp.where(is_own, own, other), 0, 1).reshape(BLK, BLK)
                    panel[(p - n) * BLK : (p - n + 1) * BLK, :] = block
                if n:
                    panel[: P_SIZE - start, :] -= dot_full(
                        lower_ref[start:, :start], lower_ref[cols, :start], 1, 1
                    )

        u, v = factor_block(panel[:BLK, :])
        upper[...] = u
        inverse_ref[k] = v
        for n in range(NPB):

            @pl.when(k == n)
            def _(n=n):
                start = n * BLK
                cols = slice(start, start + BLK)
                lower_ref[cols, cols] = upper[...].T
                if n < NPB - 1:
                    lower_ref[start + BLK :, cols] = dot_full(
                        panel[BLK : P_SIZE - start, :], inverse_ref[n], 1, 1
                    )

        return carry

    lax.fori_loop(0, NPB, step, 0)
    top_ref[...] = lower_ref[
        pl.ds(pl.multiple_of(jnp.minimum(grid_row, NPB - 1) * BLK, BLK), BLK), :
    ]
    low_hi[...], low_lo[...] = split(lower_ref[...])
    for n in range(STEPS):
        a, b = inverse_ref[2 * n], inverse_ref[2 * n + 1]
        mid = lower_ref[(2 * n + 1) * BLK : (2 * n + 2) * BLK, 2 * n * BLK : (2 * n + 1) * BLK]
        corner = -dot_full(dot_full(b, mid, 1, 0), a, 1, 0)
        whole = jnp.concatenate(
            [
                jnp.concatenate([a, jnp.zeros((BLK, BLK), F32)], 1),
                jnp.concatenate([corner, b], 1),
            ],
            0,
        )
        inv_hi[n], inv_lo[n] = split(whole)


def cholesky(where, own, other):
    bf16 = jnp.bfloat16
    whole = pl.BlockSpec(memory_space=pltpu.VMEM)
    return pl.pallas_call(
        cholesky_kernel,
        in_specs=[pl.BlockSpec(memory_space=pltpu.SMEM), whole, whole],
        out_specs=[whole] * 5,
        out_shape=[jax.ShapeDtypeStruct((P_SIZE, P_SIZE), bf16)] * 2
        + [jax.ShapeDtypeStruct((STEPS, WIDE, WIDE), bf16)] * 2
        + [jax.ShapeDtypeStruct((BLK, P_SIZE), F32)],
        scratch_shapes=[
            pltpu.VMEM((P_SIZE, P_SIZE), F32),
            pltpu.VMEM((NPB, BLK, BLK), F32),
            pltpu.VMEM((P_SIZE, BLK), F32),
            pltpu.VMEM((BLK, BLK), F32),
        ],
        compiler_params=pltpu.CompilerParams(vmem_limit_bytes=60 * 2**20),
        cost_estimate=pl.CostEstimate(
            flops=1, bytes_accessed=1, transcendentals=0
        ),
        name="cholesky",
    )(where, own, other)


def solve_strip(strip, lower, inverse, done_hi, done_lo, factor=None, ready=None):
    for n in range(STEPS):
        cols, done = slice(n * WIDE, (n + 1) * WIDE), slice(0, n * WIDE)
        part = strip[:, cols]
        if ready is not None:
            ready(n)
        if n:
            part = part - dot_split(
                (done_hi[:, done], done_lo[:, done]), (lower[0][cols, done], lower[1][cols, done])
            )
        part = dot_split(split(part), (inverse[0][n], inverse[1][n]))
        if factor is not None:
            factor[:, cols] = part
        done_hi[:, cols], done_lo[:, cols] = split(part)


def column_kernel(
    col_hbm,
    low_hi_hbm,
    low_lo_hbm,
    inv_hi_hbm,
    inv_lo_hbm,
    col_hi,
    col_lo,
    col_ref,
    low_hi,
    low_lo,
    inv_hi,
    inv_lo,
    strip,
    sems,
):
    pairs = [
        (col_hbm, col_ref),
        (inv_hi_hbm, inv_hi),
        (inv_lo_hbm, inv_lo),
        (low_hi_hbm, low_hi),
        (low_lo_hbm, low_lo),
    ]
    loads = [pltpu.make_async_copy(a, b, sems.at[n]) for n, (a, b) in enumerate(pairs)]
    for load in loads:
        load.start()
    loads[0].wait()
    for b in range(4):
        part = jnp.swapaxes(col_ref[:, :, b * NPB : (b + 1) * NPB, :], 0, 1)
        part = jnp.swapaxes(part.reshape(BLK, NPB, BLK), 0, 1)
        for q in range(NPB):
            cols = slice(q * BLK, (q + 1) * BLK)
            strip[b * BLK : (b + 1) * BLK, cols] = part[q]
    for load in loads[1:]:
        load.wait()

    solve_strip(strip, (low_hi, low_lo), (inv_hi, inv_lo), col_hi, col_lo)


def solve_columns(col_strip, *factor_parts):
    inputs = (col_strip, *factor_parts)
    anywhere = pl.BlockSpec(memory_space=pl.ANY)
    return pl.pallas_call(
        column_kernel,
        in_specs=[anywhere] * len(inputs),
        out_specs=[pl.BlockSpec(memory_space=pltpu.VMEM)] * 2,
        out_shape=[jax.ShapeDtypeStruct((STRIP, P_SIZE), jnp.bfloat16)] * 2,
        scratch_shapes=[pltpu.VMEM(x.shape, x.dtype) for x in inputs]
        + [pltpu.VMEM((STRIP, P_SIZE), F32), pltpu.SemaphoreType.DMA((len(inputs),))],
        compiler_params=pltpu.CompilerParams(vmem_limit_bytes=60 * 2**20),
        cost_estimate=pl.CostEstimate(
            flops=200_000_000_000, bytes_accessed=9_000_000, transcendentals=0
        ),
        name="solve_columns",
    )(*inputs)


def row_kernel(
    own_hbm,
    low_hi_hbm,
    low_lo_hbm,
    inv_hi_hbm,
    inv_lo_hbm,
    factor_ref,
    own_ref,
    low_hi,
    low_lo,
    inv_hi,
    inv_lo,
    strip,
    row_hi,
    row_lo,
    sems,
):
    pairs = [
        (own_hbm.at[:, 16:, :], own_ref),
        (inv_hi_hbm, inv_hi),
        (inv_lo_hbm, inv_lo),
    ]
    for n in range(1, STEPS):
        spot = (slice(n * WIDE, (n + 1) * WIDE), slice(0, n * WIDE))
        pairs += [(low_hi_hbm.at[spot], low_hi.at[spot]), (low_lo_hbm.at[spot], low_lo.at[spot])]
    loads = [pltpu.make_async_copy(a, b, sems.at[n]) for n, (a, b) in enumerate(pairs)]
    for load in loads:
        load.start()
    loads[0].wait()
    for h in range(2):
        part = jnp.swapaxes(own_ref[:, h * NPB : (h + 1) * NPB, :], 0, 1)
        for q in range(NPB):
            strip[h * BLK : (h + 1) * BLK, q * BLK : (q + 1) * BLK] = part[q]

    def ready(n):
        for load in loads[1 + 2 * n : 3 + 2 * n]:
            load.wait()

    solve_strip(strip, (low_hi, low_lo), (inv_hi, inv_lo), row_hi, row_lo, factor_ref, ready)


def solve_rows(rows_in, *factor_parts):
    anywhere = pl.BlockSpec(memory_space=pl.ANY)
    half = (STRIP // 2, P_SIZE)
    return pl.pallas_call(
        row_kernel,
        in_specs=[anywhere] * 5,
        out_specs=pl.BlockSpec(memory_space=pltpu.VMEM),
        out_shape=jax.ShapeDtypeStruct(half, F32),
        scratch_shapes=[pltpu.VMEM((BLK, 16, BLK), F32)]
        + [pltpu.VMEM(x.shape, x.dtype) for x in factor_parts]
        + [pltpu.VMEM(half, F32)]
        + [pltpu.VMEM(half, jnp.bfloat16)] * 2
        + [pltpu.SemaphoreType.DMA((9,))],
        compiler_params=pltpu.CompilerParams(vmem_limit_bytes=60 * 2**20),
        cost_estimate=pl.CostEstimate(
            flops=2_000_000_000, bytes_accessed=5_000_000, transcendentals=0
        ),
        name="solve_rows",
    )(rows_in, *factor_parts)


def front_kernel(where_ref, sums_hbm, entry_ref, front_ref, sums_ref, sem):
    grid_row, grid_col = where_ref[1], where_ref[2]
    load = pltpu.make_async_copy(sums_hbm.at[:, :16, :], sums_ref, sem)
    load.start()
    load.wait()
    for b in range(4):
        if b % 2 == 0:
            blocks = jnp.swapaxes(sums_ref[:, b * 4 : b * 4 + 8, :], 0, 1)
        for d in range(4):
            sums = blocks[b % 2 * 4 + d]
            if b < d:
                sums = sums.T
            elif b == d:
                sums = jnp.where(grid_row >= grid_col, sums, sums.T)
            entry = entry_ref[pl.ds(b * STRIP + d, BLK, stride=4), :]
            front_ref[b * BLK : (b + 1) * BLK, d * BLK : (d + 1) * BLK] = entry + sums


def assemble(where, rows_in, entries):
    whole = pl.BlockSpec(memory_space=pltpu.VMEM)
    return pl.pallas_call(
        front_kernel,
        in_specs=[
            pl.BlockSpec(memory_space=pltpu.SMEM),
            pl.BlockSpec(memory_space=pl.ANY),
            whole,
        ],
        out_specs=whole,
        out_shape=jax.ShapeDtypeStruct((STRIP, STRIP), F32),
        scratch_shapes=[pltpu.VMEM((BLK, 16, BLK), F32), pltpu.SemaphoreType.DMA(())],
        compiler_params=pltpu.CompilerParams(vmem_limit_bytes=60 * 2**20),
        cost_estimate=pl.CostEstimate(
            flops=1_000_000_000, bytes_accessed=4_000_000, transcendentals=0
        ),
        name="assemble",
    )(where, rows_in, entries)


def update_kernel(
    where_ref,
    own_hbm,
    other_hbm,
    col_hi_hbm,
    col_lo_hbm,
    front_hbm,
    top_hbm,
    factor_hbm,
    out_hbm,
    col_hi,
    col_lo,
    front_ref,
    top_ref,
    factor_ref,
    out_ref,
    product,
    sems,
):
    first_core, grid_row, grid_col = where_ref[0] == 0, where_ref[1], where_ref[2]
    pairs = [(col_hi_hbm, col_hi), (col_lo_hbm, col_lo), (front_hbm, front_ref), (top_hbm, top_ref)]
    loads = [pltpu.make_async_copy(a, b, sems.at[n]) for n, (a, b) in enumerate(pairs)]
    halves = factor_ref.at[: STRIP // 2], factor_ref.at[STRIP // 2 :]

    def load_rows(first, second):
        copies = [
            pltpu.make_async_copy(first, halves[0], sems.at[4]),
            pltpu.make_async_copy(second, halves[1], sems.at[5]),
        ]
        for copy in copies:
            copy.start()
        for load in loads:
            load.start()
        for copy in copies:
            copy.wait()

    @pl.when(first_core)
    def _():
        load_rows(own_hbm, other_hbm)

    @pl.when(jnp.logical_not(first_core))
    def _():
        load_rows(other_hbm, own_hbm)

    for load in loads:
        load.wait()

    @pl.when(grid_row < NPB)
    def _():
        factor_ref[:BLK, :] = top_ref[...]

    factor_store = pltpu.make_async_copy(factor_ref, factor_hbm, sems.at[6])
    factor_store.start()
    product[...] = dot_split(split(factor_ref[...]), (col_hi[...], col_lo[...]))
    for b in range(4):
        for d in range(4):
            rows, cols = slice(b * BLK, (b + 1) * BLK), slice(d * BLK, (d + 1) * BLK)
            trail = product[rows, cols]
            if b == 0:
                trail = jnp.where(grid_row >= NPB, trail, 0.0)
            if d == 0:
                trail = jnp.where(grid_col >= NPB, trail, 0.0)
            out_ref[pl.ds(b * STRIP + d, BLK, stride=4), :] = front_ref[rows, cols] - trail
    out_store = pltpu.make_async_copy(out_ref, out_hbm, sems.at[7])
    out_store.start()
    factor_store.wait()
    out_store.wait()


def update(where, own, other, columns, front, top):
    inputs = (own, other, *columns, front, top)
    outputs = [
        jax.ShapeDtypeStruct((STRIP, P_SIZE), F32),
        jax.ShapeDtypeStruct((4 * STRIP, BLK), F32),
    ]
    anywhere = pl.BlockSpec(memory_space=pl.ANY)
    return pl.pallas_call(
        update_kernel,
        in_specs=[pl.BlockSpec(memory_space=pltpu.SMEM)] + [anywhere] * len(inputs),
        out_specs=[anywhere] * 2,
        out_shape=outputs,
        scratch_shapes=[pltpu.VMEM(x.shape, x.dtype) for x in (*inputs[2:], *outputs)]
        + [pltpu.VMEM((STRIP, STRIP), F32), pltpu.SemaphoreType.DMA((8,))],
        compiler_params=pltpu.CompilerParams(vmem_limit_bytes=60 * 2**20),
        cost_estimate=pl.CostEstimate(
            flops=2_000_000_000, bytes_accessed=9_000_000, transcendentals=0
        ),
        name="update",
    )(where, *inputs)


def split_kernel(counts, child_ref, entry_ref, out_ref):
    sources = [(child_ref, 6 * BLK * b + d, 6) for b, n in enumerate(counts) for d in range(n)]
    sources += [(entry_ref, STRIP * b, 4) for b in range(4)]
    for slot, (ref, start, stride) in enumerate(sources):
        out_ref[pl.ds(slot, BLK, stride=16), :] = ref[pl.ds(start, BLK, stride=stride), :]


def split_blocks(counts, child, entries):
    whole = pl.BlockSpec(memory_space=pltpu.VMEM)
    return pl.pallas_call(
        functools.partial(split_kernel, counts),
        in_specs=[whole] * 2,
        out_specs=whole,
        out_shape=jax.ShapeDtypeStruct((BLK * 16, BLK), F32),
        compiler_params=pltpu.CompilerParams(vmem_limit_bytes=60 * 2**20),
        cost_estimate=pl.CostEstimate(flops=0, bytes_accessed=3_000_000, transcendentals=0),
        name="split_blocks",
    )(child, entries)


def pack_kernel(inverse_map_ref, own_ref, other_ref, panel_ref, out_ref):
    for p in range(FB):
        b, r = divmod(p, GR)
        total = jnp.zeros((4 * NC, BLK), F32)
        for k, child in enumerate((own_ref, other_ref)):
            spot = inverse_map_ref[k, p]
            total = total + jnp.where(spot >= 0, child[jnp.maximum(spot, 0)], 0.0)
        for d in range(4):
            out_ref[pl.ds(r * 32 + b * 4 + d, NC, stride=GR * 32), :] = total[d * NC : (d + 1) * NC]
    for h in range(2):
        for r in range(GR):
            rows = panel_ref[h, r]
            for c in range(NC):
                out_ref[pl.ds((c * GR + r) * 32 + 16 + h * 8, NPB), :] = rows


def pack(inverse_maps, own, other, panel):
    whole = pl.BlockSpec(memory_space=pltpu.VMEM)
    return pl.pallas_call(
        pack_kernel,
        in_specs=[pl.BlockSpec(memory_space=pltpu.SMEM)] + [whole] * 3,
        out_specs=whole,
        out_shape=jax.ShapeDtypeStruct((CHIPS * 32, BLK), F32),
        compiler_params=pltpu.CompilerParams(vmem_limit_bytes=12 * 2**20),
        cost_estimate=pl.CostEstimate(flops=0, bytes_accessed=8_000_000, transcendentals=0),
        name="pack",
    )(inverse_maps, own, other, panel)


def to_chips(x):
    return lax.all_to_all(x, ("col", "row"), 0, 0)


def after(x, earlier):
    return lax.optimization_barrier((x, earlier))[0]


def swap_cores(x):
    return lax.ppermute(x, "sub", [(0, 1), (1, 0)])


def per_device(front_entries, child_updates, row_maps):
    my_row = lax.axis_index("row")
    my_col = lax.axis_index("col")
    my_sub = lax.axis_index("sub")
    entries = front_entries[:, 0, :, :, 0, :]
    child_own = child_updates[0, :, 0, :, :, 0, :]
    own_map = lax.dynamic_index_in_dim(row_maps, my_sub, 0, keepdims=False)
    other_map = lax.dynamic_index_in_dim(row_maps, 1 - my_sub, 0, keepdims=False)
    blocks = jnp.arange(FB, dtype=jnp.int32)
    where = jnp.stack([my_sub, my_row, my_sub * NC + my_col]).astype(jnp.int32)

    counts = [2 * b + 2 for b in range(3)]
    entries = entries.reshape(4 * STRIP, BLK)
    slices_out = split_blocks(counts, child_own.reshape(18 * BLK, BLK), entries)
    slices_out = slices_out.reshape(CHIPS, 16, BLK)
    slices_in = to_chips(slices_out).reshape(NC, GR, 16, BLK)
    lower_child, start = [], 0
    for count in counts:
        part = slices_in[:, :, start : start + count].transpose(1, 2, 0, 3)
        part = jnp.pad(part, ((0, 0), (0, 6 - count), (0, 0), (0, 0)))
        lower_child.append(part.reshape(GR, UB, BLK))
        start += count
    lower_child = jnp.concatenate(lower_child, 0)
    entry_rows = slices_in[:, :, start:].transpose(2, 1, 0, 3).reshape(FB, NPB, BLK)

    row_pick = (own_map[None, :] == blocks[:, None]).astype(F32)
    col_pick = (own_map[None, :NPB] == blocks[:NPB, None]).astype(F32)
    both_pick = (row_pick[:, None, :, None] * col_pick[None, :, None, :]).reshape(
        FB * NPB, UB * NPB
    )
    child_panel = lower_child[:, :NPB].reshape(UB * NPB, BLK)
    placed = dot_full(both_pick, child_panel, 1, 0).reshape(FB, NPB, BLK)
    placed = placed + jnp.where(my_sub == 0, entry_rows, 0.0)
    panel_rows = placed + swap_cores(placed)

    by_grid = panel_rows.reshape(4, 2, NC, NPB, BLK)
    for_cols = lax.dynamic_index_in_dim(by_grid, my_sub, 1, keepdims=False).transpose(1, 0, 2, 3)
    triangle = jnp.concatenate([panel_rows[q:NPB, q] for q in range(NPB)], 0)
    triangle = lax.dynamic_index_in_dim(triangle.reshape(2, HALF, BLK), my_sub, 0, False)
    triangle = jnp.broadcast_to(triangle[None], (NC, HALF, BLK))
    along_col = lax.all_to_all(
        jnp.concatenate([for_cols.reshape(NC, 32, BLK), triangle], 1), "col", 0, 0
    )
    col_part = along_col[:, :32]
    lead = along_col[:, 32:].transpose(1, 0, 2).reshape(HALF * 8, BLK)
    lead = after(lead, col_part)
    lead = lax.all_to_all(jnp.broadcast_to(lead[None], (GR, HALF * 8, BLK)), "row", 0, 0)

    ids = jnp.arange(UB, dtype=jnp.int32)
    below = (ids[:, None] > ids[None, :])[:, :, None]
    on_or_below = (ids[:, None] >= ids[None, :])[:, :, None]
    lower_child = after(lower_child, along_col)
    child = jnp.where(on_or_below, lower_child, 0.0)
    child = child + jnp.where(below, lower_child, 0.0).transpose(1, 0, 2)
    col_ids = blocks.reshape(4, 2, NC)
    own_cols = lax.dynamic_index_in_dim(col_ids, my_sub, 1, keepdims=False).reshape(-1)
    other_cols = lax.dynamic_index_in_dim(col_ids, 1 - my_sub, 1, keepdims=False).reshape(-1)
    all_cols = jnp.concatenate([own_cols, other_cols])
    widen = (own_map[None, :] == all_cols[:, None]).astype(F32)
    widened = jnp.einsum("qj,ijl->iql", widen, child, precision=HIGHEST)
    kept, arrived = widened[:, : FB // 2], swap_cores(widened[:, FB // 2 :])

    both_maps = jnp.stack([own_map, other_map])
    hit = both_maps[:, None, :] == blocks[None, :, None]
    inverse_maps = jnp.max(jnp.where(hit, ids, -1), axis=2)
    halves = panel_rows.reshape(2, 2, GR, NPB, BLK)
    for_rows = lax.dynamic_index_in_dim(halves, my_sub, 0, keepdims=False)
    rows_out = pack(inverse_maps, kept, arrived, for_rows).reshape(CHIPS, 32, BLK)
    lead, rows_out = lax.optimization_barrier((lead, rows_out))
    other_lead = swap_cores(lead)
    col_strip = lax.all_gather(after(col_part, lead), "row", axis=0)
    rows_in = to_chips(rows_out)

    *factor_parts, top = cholesky(where, lead, other_lead)
    columns = solve_columns(col_strip, *factor_parts)
    rows_in = after(rows_in, columns[0])
    own_rows = solve_rows(rows_in, *factor_parts)
    other_rows = swap_cores(own_rows)
    front = assemble(where, rows_in, after(entries, own_rows))
    factor, updated = update(where, own_rows, other_rows, columns, front, top)
    updated = updated.reshape(4, 1, BLK, 4, 1, BLK)
    return updated, factor.reshape(4, 1, BLK, P_SIZE)


def solution(mesh):
    in_specs = (
        P(None, "row", None, None, ("sub", "col"), None),
        P("sub", None, "row", None, None, "col", None),
        P(),
    )
    out_specs = (P(None, "row", None, None, ("sub", "col"), None), P(None, "row", None, None))
    return jax.shard_map(
        per_device, mesh=mesh, in_specs=in_specs, out_specs=out_specs, check_vma=False
    )
```

```python
import functools

import jax
import jax.numpy as jnp
from jax import lax
from jax.experimental import pallas as pl
from jax.experimental.pallas import tpu as pltpu
from jax.sharding import PartitionSpec as P

BLK = 128
FB = 64
UB = 48
P_SIZE = 1024
NPB = 8
GR = 16
NC = 8
CHIPS = GR * NC
F32 = jnp.float32
HIGHEST = lax.Precision.HIGHEST


def dot_full(a, b, dim_a, dim_b):
    return lax.dot_general(
        a, b, (((dim_a,), (dim_b,)), ((), ())), precision=HIGHEST, preferred_element_type=F32
    )


def split(x):
    high = x.astype(jnp.bfloat16)
    return high, (x - high.astype(F32)).astype(jnp.bfloat16)


def dot_split(a, b):
    def dot(x, y):
        return lax.dot_general(x, y, (((1,), (1,)), ((), ())), preferred_element_type=F32)

    return dot(a[0], b[0]) + (dot(a[0], b[1]) + dot(a[1], b[0]))


def split_rows(x):
    def head(y):
        return y.astype(jnp.bfloat16).astype(F32)

    high = head(x)
    mid = head(x - high)
    return high, mid, head(x - high - mid)


def stacked(parts):
    return jnp.concatenate(parts, 0).astype(jnp.bfloat16)


def reciprocal(x):
    guess = pltpu.reciprocal(x, approx=True)
    return guess * (2.0 - x * guess)


def row_of(x, t):
    return jnp.broadcast_to(x[t : t + 1, :], x.shape)


def col_of(x, t):
    return jnp.broadcast_to(x[:, t : t + 1], x.shape)


def products(columns, rows):
    parts = [c * r for c, r in zip(columns, rows, strict=True)]
    while len(parts) > 1:
        parts = [parts[2 * n] + parts[2 * n + 1] for n in range(len(parts) // 2)]
    return parts[0]


NEAR = 2


def factor_block(w):
    sub = lax.broadcasted_iota(jnp.int32, (8, BLK), 0)
    lane = lax.broadcasted_iota(jnp.int32, (8, BLK), 1)
    tiles = BLK // 8
    left = [w[8 * i : 8 * i + 8, :] for i in range(tiles)]
    right = [(lane == sub + 8 * i).astype(F32) for i in range(tiles)]
    uppers, inverses = [], []
    diag = [col_of(left[0], t) for t in range(8)]
    for s in range(tiles):
        rows, extra = left[s], right[s]
        raw, last = rows, s == tiles - 1
        ahead, later, near = [], [], {}
        if not last:
            ahead = [col_of(rows, 8 * s + 8 + t) for t in range(8)]
            later = [col_of(left[s + 1], 8 * s + 8 + t) for t in range(8)]
            near = {
                i: [col_of(left[i], 8 * s + t) for t in range(8)]
                for i in range(s + 1, min(tiles, s + 1 + NEAR))
            }
        u, v, pivots = rows, extra, None
        for t in range(0, 8, 2):
            c0, c1 = diag[t], diag[t + 1]
            a, b, d = row_of(c0, t), row_of(c1, t), row_of(c1, t + 1)
            inv_det = reciprocal(a * d - b * b)
            at0, at1 = sub == t, sub == t + 1
            either = at0 | at1
            g0 = jnp.where(at0, -d, jnp.where(at1, b, c0 * d - c1 * b))
            g1 = jnp.where(at0, b, jnp.where(at1, -a, c1 * a - c0 * b))
            h0, h1 = g0 * inv_det, g1 * inv_det
            ratio = b * reciprocal(a)
            u = jnp.where(at0, rows, jnp.where(at1, row_of(rows, t + 1) - ratio * row_of(rows, t), u))
            v = jnp.where(
                at0, extra, jnp.where(at1, row_of(extra, t + 1) - ratio * row_of(extra, t), v)
            )
            pivots = a if pivots is None else jnp.where(at0, a, pivots)
            pivots = jnp.where(at1, d - b * ratio, pivots)

            def reduce(x, soon=False):
                x0, x1, base = row_of(x, t), row_of(x, t + 1), jnp.where(either, 0.0, x)
                if soon:
                    return base - (g0 * x0 + g1 * x1) * inv_det
                return base - (h0 * x0 + h1 * x1)

            for c in range(t + 2, 8):
                diag[c] = reduce(diag[c], c < t + 4)
            ahead = [reduce(x) for x in ahead]
            rows, extra = reduce(rows), reduce(extra)
        scale = lax.rsqrt(pivots)
        uppers.append(jnp.where(lane >= sub + 8 * s, u * scale, 0.0))
        inverses.append(v * scale)
        if last:
            break
        diag = [
            later[c] - products(near[s + 1], [row_of(ahead[c], t) for t in range(8)])
            for c in range(8)
        ]
        row_terms = [row_of(rows, t) for t in range(8)]
        extra_terms = [row_of(extra, t) for t in range(8)]
        for i, columns in near.items():
            left[i] = left[i] - products(columns, row_terms)
            right[i] = right[i] - products(columns, extra_terms)
        if s + 1 + NEAR < tiles:
            high, mid, low = split_rows(raw)
            far_columns = stacked([high, high, mid, mid, high, low])
            high, mid, low = split_rows(jnp.concatenate([rows, extra], 1))
            far_rows = stacked([high, mid, high, mid, low, high])
            far = lax.dot_general(
                far_columns, far_rows, (((0,), (0,)), ((), ())), preferred_element_type=F32
            )
            for i in range(s + 1 + NEAR, tiles):
                left[i] = left[i] - far[8 * i : 8 * i + 8, :BLK]
                right[i] = right[i] - far[8 * i : 8 * i + 8, BLK:]
    return jnp.concatenate(uppers, 0), jnp.concatenate(inverses, 0)


WIDE = 2 * BLK
STRIP = 4 * BLK
STEPS = P_SIZE // WIDE
TRIANGLE = [(p, q) for q in range(NPB) for p in range(q, NPB)]
HALF = len(TRIANGLE) // 2


def cholesky_kernel(
    where_ref,
    own_ref,
    other_ref,
    low_hi,
    low_lo,
    inv_hi,
    inv_lo,
    top_ref,
    lower_ref,
    inverse_ref,
    panel,
    upper,
):
    first_core, grid_row = where_ref[0] == 0, where_ref[1]
    lower_ref[...] = jnp.zeros_like(lower_ref)

    def step(k, carry):
        for n in range(NPB):

            @pl.when(k == n)
            def _(n=n):
                start = n * BLK
                cols = slice(start, start + BLK)
                for p in range(n, NPB):
                    spot = TRIANGLE.index((p, n))
                    rows = slice(spot % HALF * 8, spot % HALF * 8 + 8)
                    own, other = own_ref[:, rows, :], other_ref[:, rows, :]
                    is_own = first_core if spot < HALF else jnp.logical_not(first_core)
                    block = jnp.swapaxes(jnp.where(is_own, own, other), 0, 1).reshape(BLK, BLK)
                    panel[(p - n) * BLK : (p - n + 1) * BLK, :] = block
                if n:
                    panel[: P_SIZE - start, :] -= dot_full(
                        lower_ref[start:, :start], lower_ref[cols, :start], 1, 1
                    )

        u, v = factor_block(panel[:BLK, :])
        upper[...] = u
        inverse_ref[k] = v
        for n in range(NPB):

            @pl.when(k == n)
            def _(n=n):
                start = n * BLK
                cols = slice(start, start + BLK)
                lower_ref[cols, cols] = upper[...].T
                if n < NPB - 1:
                    lower_ref[start + BLK :, cols] = dot_full(
                        panel[BLK : P_SIZE - start, :], inverse_ref[n], 1, 1
                    )

        return carry

    lax.fori_loop(0, NPB, step, 0)
    top_ref[...] = lower_ref[
        pl.ds(pl.multiple_of(jnp.minimum(grid_row, NPB - 1) * BLK, BLK), BLK), :
    ]
    low_hi[...], low_lo[...] = split(lower_ref[WIDE:, : P_SIZE - WIDE])
    for n in range(STEPS):
        a, b = inverse_ref[2 * n], inverse_ref[2 * n + 1]
        mid = lower_ref[(2 * n + 1) * BLK : (2 * n + 2) * BLK, 2 * n * BLK : (2 * n + 1) * BLK]
        corner = -dot_full(dot_full(b, mid, 1, 0), a, 1, 0)
        whole = jnp.concatenate(
            [
                jnp.concatenate([a, jnp.zeros((BLK, BLK), F32)], 1),
                jnp.concatenate([corner, b], 1),
            ],
            0,
        )
        inv_hi[n], inv_lo[n] = split(whole)


def cholesky(where, own, other):
    bf16 = jnp.bfloat16
    whole = pl.BlockSpec(memory_space=pltpu.VMEM)
    return pl.pallas_call(
        cholesky_kernel,
        in_specs=[pl.BlockSpec(memory_space=pltpu.SMEM), whole, whole],
        out_specs=[whole] * 5,
        out_shape=[jax.ShapeDtypeStruct((P_SIZE - WIDE, P_SIZE - WIDE), bf16)] * 2
        + [jax.ShapeDtypeStruct((STEPS, WIDE, WIDE), bf16)] * 2
        + [jax.ShapeDtypeStruct((BLK, P_SIZE), F32)],
        scratch_shapes=[
            pltpu.VMEM((P_SIZE, P_SIZE), F32),
            pltpu.VMEM((NPB, BLK, BLK), F32),
            pltpu.VMEM((P_SIZE, BLK), F32),
            pltpu.VMEM((BLK, BLK), F32),
        ],
        compiler_params=pltpu.CompilerParams(vmem_limit_bytes=60 * 2**20),
        cost_estimate=pl.CostEstimate(
            flops=1, bytes_accessed=1, transcendentals=0
        ),
        name="cholesky",
    )(where, own, other)


def solve_strip(strip, lower, inverse, done_hi, done_lo, factor=None, ready=None):
    for n in range(STEPS):
        cols, done = slice(n * WIDE, (n + 1) * WIDE), slice(0, n * WIDE)
        above = slice((n - 1) * WIDE, n * WIDE)
        part = strip[:, cols]
        if ready is not None:
            ready(n)
        if n:
            part = part - dot_split(
                (done_hi[:, done], done_lo[:, done]), (lower[0][above, done], lower[1][above, done])
            )
        part = dot_split(split(part), (inverse[0][n], inverse[1][n]))
        if factor is not None:
            factor[:, cols] = part
        done_hi[:, cols], done_lo[:, cols] = split(part)


def start_loads(strip_hbm, strip_ref, parts, sems):
    pairs = [(strip_hbm, strip_ref), *parts[2:]]
    for n in range(1, STEPS):
        spot = (slice((n - 1) * WIDE, n * WIDE), slice(0, n * WIDE))
        pairs += [(source.at[spot], target.at[spot]) for source, target in parts[:2]]
    loads = [pltpu.make_async_copy(a, b, sems.at[n]) for n, (a, b) in enumerate(pairs)]
    for load in loads:
        load.start()

    def ready(n):
        for load in loads[1 + 2 * n : 3 + 2 * n]:
            load.wait()

    return loads[0], ready


def column_kernel(
    col_hbm,
    low_hi_hbm,
    low_lo_hbm,
    inv_hi_hbm,
    inv_lo_hbm,
    col_hi,
    col_lo,
    col_ref,
    low_hi,
    low_lo,
    inv_hi,
    inv_lo,
    strip,
    sems,
):
    parts = ((low_hi_hbm, low_hi), (low_lo_hbm, low_lo), (inv_hi_hbm, inv_hi), (inv_lo_hbm, inv_lo))
    first, ready = start_loads(col_hbm, col_ref, parts, sems)
    first.wait()
    for b in range(4):
        part = jnp.swapaxes(col_ref[:, :, b * NPB : (b + 1) * NPB, :], 0, 1)
        part = jnp.swapaxes(part.reshape(BLK, NPB, BLK), 0, 1)
        for q in range(NPB):
            cols = slice(q * BLK, (q + 1) * BLK)
            strip[b * BLK : (b + 1) * BLK, cols] = part[q]
    solve_strip(strip, (low_hi, low_lo), (inv_hi, inv_lo), col_hi, col_lo, None, ready)


def solve_columns(col_strip, *factor_parts):
    inputs = (col_strip, *factor_parts)
    anywhere = pl.BlockSpec(memory_space=pl.ANY)
    return pl.pallas_call(
        column_kernel,
        in_specs=[anywhere] * len(inputs),
        out_specs=[pl.BlockSpec(memory_space=pltpu.VMEM)] * 2,
        out_shape=[jax.ShapeDtypeStruct((STRIP, P_SIZE), jnp.bfloat16)] * 2,
        scratch_shapes=[pltpu.VMEM(x.shape, x.dtype) for x in inputs]
        + [pltpu.VMEM((STRIP, P_SIZE), F32), pltpu.SemaphoreType.DMA((9,))],
        compiler_params=pltpu.CompilerParams(vmem_limit_bytes=60 * 2**20),
        cost_estimate=pl.CostEstimate(
            flops=200_000_000_000, bytes_accessed=9_000_000, transcendentals=0
        ),
        name="solve_columns",
    )(*inputs)


def row_kernel(
    own_hbm,
    low_hi_hbm,
    low_lo_hbm,
    inv_hi_hbm,
    inv_lo_hbm,
    factor_ref,
    own_ref,
    low_hi,
    low_lo,
    inv_hi,
    inv_lo,
    strip,
    row_hi,
    row_lo,
    sems,
):
    parts = ((low_hi_hbm, low_hi), (low_lo_hbm, low_lo), (inv_hi_hbm, inv_hi), (inv_lo_hbm, inv_lo))
    first, ready = start_loads(own_hbm.at[:, 16:, :], own_ref, parts, sems)
    first.wait()
    for h in range(2):
        part = jnp.swapaxes(own_ref[:, h * NPB : (h + 1) * NPB, :], 0, 1)
        for q in range(NPB):
            strip[h * BLK : (h + 1) * BLK, q * BLK : (q + 1) * BLK] = part[q]

    solve_strip(strip, (low_hi, low_lo), (inv_hi, inv_lo), row_hi, row_lo, factor_ref, ready)


def solve_rows(rows_in, *factor_parts):
    anywhere = pl.BlockSpec(memory_space=pl.ANY)
    half = (STRIP // 2, P_SIZE)
    return pl.pallas_call(
        row_kernel,
        in_specs=[anywhere] * 5,
        out_specs=pl.BlockSpec(memory_space=pltpu.VMEM),
        out_shape=jax.ShapeDtypeStruct(half, F32),
        scratch_shapes=[pltpu.VMEM((BLK, 16, BLK), F32)]
        + [pltpu.VMEM(x.shape, x.dtype) for x in factor_parts]
        + [pltpu.VMEM(half, F32)]
        + [pltpu.VMEM(half, jnp.bfloat16)] * 2
        + [pltpu.SemaphoreType.DMA((9,))],
        compiler_params=pltpu.CompilerParams(vmem_limit_bytes=60 * 2**20),
        cost_estimate=pl.CostEstimate(
            flops=2_000_000_000, bytes_accessed=5_000_000, transcendentals=0
        ),
        name="solve_rows",
    )(rows_in, *factor_parts)


def front_kernel(where_ref, sums_hbm, entry_ref, front_ref, sums_ref, sem):
    grid_row, grid_col = where_ref[1], where_ref[2]
    load = pltpu.make_async_copy(sums_hbm.at[:, :16, :], sums_ref, sem)
    load.start()
    load.wait()
    for b in range(4):
        if b % 2 == 0:
            blocks = jnp.swapaxes(sums_ref[:, b * 4 : b * 4 + 8, :], 0, 1)
        for d in range(4):
            sums = blocks[b % 2 * 4 + d]
            if b < d:
                sums = sums.T
            elif b == d:
                sums = jnp.where(grid_row >= grid_col, sums, sums.T)
            entry = entry_ref[pl.ds(b * STRIP + d, BLK, stride=4), :]
            front_ref[b * BLK : (b + 1) * BLK, d * BLK : (d + 1) * BLK] = entry + sums


def assemble(where, rows_in, entries):
    whole = pl.BlockSpec(memory_space=pltpu.VMEM)
    return pl.pallas_call(
        front_kernel,
        in_specs=[
            pl.BlockSpec(memory_space=pltpu.SMEM),
            pl.BlockSpec(memory_space=pl.ANY),
            whole,
        ],
        out_specs=whole,
        out_shape=jax.ShapeDtypeStruct((STRIP, STRIP), F32),
        scratch_shapes=[pltpu.VMEM((BLK, 16, BLK), F32), pltpu.SemaphoreType.DMA(())],
        compiler_params=pltpu.CompilerParams(vmem_limit_bytes=60 * 2**20),
        cost_estimate=pl.CostEstimate(
            flops=1_000_000_000, bytes_accessed=4_000_000, transcendentals=0
        ),
        name="assemble",
    )(where, rows_in, entries)


def update_kernel(
    where_ref,
    own_hbm,
    other_hbm,
    col_hi_hbm,
    col_lo_hbm,
    front_hbm,
    top_hbm,
    factor_hbm,
    out_hbm,
    col_hi,
    col_lo,
    front_ref,
    top_ref,
    factor_ref,
    out_ref,
    product,
    sems,
):
    first_core, grid_row, grid_col = where_ref[0] == 0, where_ref[1], where_ref[2]
    pairs = [(col_hi_hbm, col_hi), (col_lo_hbm, col_lo), (front_hbm, front_ref), (top_hbm, top_ref)]
    loads = [pltpu.make_async_copy(a, b, sems.at[n]) for n, (a, b) in enumerate(pairs)]
    halves = factor_ref.at[: STRIP // 2], factor_ref.at[STRIP // 2 :]

    def load_rows(first, second):
        copies = [
            pltpu.make_async_copy(first, halves[0], sems.at[4]),
            pltpu.make_async_copy(second, halves[1], sems.at[5]),
        ]
        for copy in copies:
            copy.start()
        for load in loads:
            load.start()
        for copy in copies:
            copy.wait()

    @pl.when(first_core)
    def _():
        load_rows(own_hbm, other_hbm)

    @pl.when(jnp.logical_not(first_core))
    def _():
        load_rows(other_hbm, own_hbm)

    for load in loads:
        load.wait()

    @pl.when(grid_row < NPB)
    def _():
        factor_ref[:BLK, :] = top_ref[...]

    factor_store = pltpu.make_async_copy(factor_ref, factor_hbm, sems.at[6])
    factor_store.start()
    product[...] = dot_split(split(factor_ref[...]), (col_hi[...], col_lo[...]))
    for b in range(4):
        for d in range(4):
            rows, cols = slice(b * BLK, (b + 1) * BLK), slice(d * BLK, (d + 1) * BLK)
            trail = product[rows, cols]
            if b == 0:
                trail = jnp.where(grid_row >= NPB, trail, 0.0)
            if d == 0:
                trail = jnp.where(grid_col >= NPB, trail, 0.0)
            out_ref[pl.ds(b * STRIP + d, BLK, stride=4), :] = front_ref[rows, cols] - trail
    out_store = pltpu.make_async_copy(out_ref, out_hbm, sems.at[7])
    out_store.start()
    factor_store.wait()
    out_store.wait()


def update(where, own, other, columns, front, top):
    inputs = (own, other, *columns, front, top)
    outputs = [
        jax.ShapeDtypeStruct((STRIP, P_SIZE), F32),
        jax.ShapeDtypeStruct((4 * STRIP, BLK), F32),
    ]
    anywhere = pl.BlockSpec(memory_space=pl.ANY)
    return pl.pallas_call(
        update_kernel,
        in_specs=[pl.BlockSpec(memory_space=pltpu.SMEM)] + [anywhere] * len(inputs),
        out_specs=[anywhere] * 2,
        out_shape=outputs,
        scratch_shapes=[pltpu.VMEM(x.shape, x.dtype) for x in (*inputs[2:], *outputs)]
        + [pltpu.VMEM((STRIP, STRIP), F32), pltpu.SemaphoreType.DMA((8,))],
        compiler_params=pltpu.CompilerParams(vmem_limit_bytes=60 * 2**20),
        cost_estimate=pl.CostEstimate(
            flops=2_000_000_000, bytes_accessed=9_000_000, transcendentals=0
        ),
        name="update",
    )(where, *inputs)


def split_kernel(counts, child_ref, entry_ref, out_ref):
    sources = [(child_ref, 6 * BLK * b + d, 6) for b, n in enumerate(counts) for d in range(n)]
    sources += [(entry_ref, STRIP * b, 4) for b in range(4)]
    for slot, (ref, start, stride) in enumerate(sources):
        out_ref[pl.ds(slot, BLK, stride=16), :] = ref[pl.ds(start, BLK, stride=stride), :]


def split_blocks(counts, child, entries):
    whole = pl.BlockSpec(memory_space=pltpu.VMEM)
    return pl.pallas_call(
        functools.partial(split_kernel, counts),
        in_specs=[whole] * 2,
        out_specs=whole,
        out_shape=jax.ShapeDtypeStruct((BLK * 16, BLK), F32),
        compiler_params=pltpu.CompilerParams(vmem_limit_bytes=60 * 2**20),
        cost_estimate=pl.CostEstimate(flops=0, bytes_accessed=3_000_000, transcendentals=0),
        name="split_blocks",
    )(child, entries)


def pack_kernel(inverse_map_ref, own_ref, other_ref, panel_ref, out_ref):
    for p in range(FB):
        b, r = divmod(p, GR)
        total = jnp.zeros((4 * NC, BLK), F32)
        for k, child in enumerate((own_ref, other_ref)):
            spot = inverse_map_ref[k, p]
            total = total + jnp.where(spot >= 0, child[jnp.maximum(spot, 0)], 0.0)
        for d in range(4):
            out_ref[pl.ds(r * 32 + b * 4 + d, NC, stride=GR * 32), :] = total[d * NC : (d + 1) * NC]
    for h in range(2):
        for r in range(GR):
            rows = panel_ref[h, r]
            for c in range(NC):
                out_ref[pl.ds((c * GR + r) * 32 + 16 + h * 8, NPB), :] = rows


def pack(inverse_maps, own, other, panel):
    whole = pl.BlockSpec(memory_space=pltpu.VMEM)
    return pl.pallas_call(
        pack_kernel,
        in_specs=[pl.BlockSpec(memory_space=pltpu.SMEM)] + [whole] * 3,
        out_specs=whole,
        out_shape=jax.ShapeDtypeStruct((CHIPS * 32, BLK), F32),
        compiler_params=pltpu.CompilerParams(vmem_limit_bytes=12 * 2**20),
        cost_estimate=pl.CostEstimate(flops=0, bytes_accessed=8_000_000, transcendentals=0),
        name="pack",
    )(inverse_maps, own, other, panel)


def to_chips(x):
    return lax.all_to_all(x, ("col", "row"), 0, 0)


def after(x, earlier):
    return lax.optimization_barrier((x, earlier))[0]


def swap_cores(x):
    return lax.ppermute(x, "sub", [(0, 1), (1, 0)])


def per_device(front_entries, child_updates, row_maps):
    my_row = lax.axis_index("row")
    my_col = lax.axis_index("col")
    my_sub = lax.axis_index("sub")
    entries = front_entries[:, 0, :, :, 0, :]
    child_own = child_updates[0, :, 0, :, :, 0, :]
    own_map = lax.dynamic_index_in_dim(row_maps, my_sub, 0, keepdims=False)
    other_map = lax.dynamic_index_in_dim(row_maps, 1 - my_sub, 0, keepdims=False)
    blocks = jnp.arange(FB, dtype=jnp.int32)
    where = jnp.stack([my_sub, my_row, my_sub * NC + my_col]).astype(jnp.int32)

    counts = [2 * b + 2 for b in range(3)]
    entries = entries.reshape(4 * STRIP, BLK)
    slices_out = split_blocks(counts, child_own.reshape(18 * BLK, BLK), entries)
    slices_out = slices_out.reshape(CHIPS, 16, BLK)
    slices_in = to_chips(slices_out).reshape(NC, GR, 16, BLK)
    lower_child, start = [], 0
    for count in counts:
        part = slices_in[:, :, start : start + count].transpose(1, 2, 0, 3)
        part = jnp.pad(part, ((0, 0), (0, 6 - count), (0, 0), (0, 0)))
        lower_child.append(part.reshape(GR, UB, BLK))
        start += count
    lower_child = jnp.concatenate(lower_child, 0)
    entry_rows = slices_in[:, :, start:].transpose(2, 1, 0, 3).reshape(FB, NPB, BLK)

    row_pick = (own_map[None, :] == blocks[:, None]).astype(F32)
    col_pick = (own_map[None, :NPB] == blocks[:NPB, None]).astype(F32)
    both_pick = (row_pick[:, None, :, None] * col_pick[None, :, None, :]).reshape(
        FB * NPB, UB * NPB
    )
    child_panel = lower_child[:, :NPB].reshape(UB * NPB, BLK)
    placed = dot_full(both_pick, child_panel, 1, 0).reshape(FB, NPB, BLK)
    placed = placed + jnp.where(my_sub == 0, entry_rows, 0.0)
    panel_rows = placed + swap_cores(placed)

    by_grid = panel_rows.reshape(4, 2, NC, NPB, BLK)
    for_cols = lax.dynamic_index_in_dim(by_grid, my_sub, 1, keepdims=False).transpose(1, 0, 2, 3)
    triangle = jnp.concatenate([panel_rows[q:NPB, q] for q in range(NPB)], 0)
    triangle = lax.dynamic_index_in_dim(triangle.reshape(2, HALF, BLK), my_sub, 0, False)
    triangle = jnp.broadcast_to(triangle[None], (NC, HALF, BLK))
    along_col = lax.all_to_all(
        jnp.concatenate([for_cols.reshape(NC, 32, BLK), triangle], 1), "col", 0, 0
    )
    col_part = along_col[:, :32]
    lead = along_col[:, 32:].transpose(1, 0, 2).reshape(HALF * 8, BLK)
    lead = after(lead, col_part)
    lead = lax.all_to_all(jnp.broadcast_to(lead[None], (GR, HALF * 8, BLK)), "row", 0, 0)

    ids = jnp.arange(UB, dtype=jnp.int32)
    below = (ids[:, None] > ids[None, :])[:, :, None]
    on_or_below = (ids[:, None] >= ids[None, :])[:, :, None]
    lower_child = after(lower_child, along_col)
    child = jnp.where(on_or_below, lower_child, 0.0)
    child = child + jnp.where(below, lower_child, 0.0).transpose(1, 0, 2)
    col_ids = blocks.reshape(4, 2, NC)
    own_cols = lax.dynamic_index_in_dim(col_ids, my_sub, 1, keepdims=False).reshape(-1)
    other_cols = lax.dynamic_index_in_dim(col_ids, 1 - my_sub, 1, keepdims=False).reshape(-1)
    all_cols = jnp.concatenate([own_cols, other_cols])
    widen = (own_map[None, :] == all_cols[:, None]).astype(F32)
    widened = jnp.einsum("qj,ijl->iql", widen, child, precision=HIGHEST)
    kept, arrived = widened[:, : FB // 2], swap_cores(widened[:, FB // 2 :])

    both_maps = jnp.stack([own_map, other_map])
    hit = both_maps[:, None, :] == blocks[None, :, None]
    inverse_maps = jnp.max(jnp.where(hit, ids, -1), axis=2)
    halves = panel_rows.reshape(2, 2, GR, NPB, BLK)
    for_rows = lax.dynamic_index_in_dim(halves, my_sub, 0, keepdims=False)
    rows_out = pack(inverse_maps, kept, arrived, for_rows).reshape(CHIPS, 32, BLK)
    lead, rows_out = lax.optimization_barrier((lead, rows_out))
    other_lead = swap_cores(lead)
    col_strip = lax.all_gather(after(col_part, lead), "row", axis=0)
    rows_in = to_chips(rows_out)

    *factor_parts, top = cholesky(where, lead, other_lead)
    columns = solve_columns(col_strip, *factor_parts)
    rows_in = after(rows_in, columns[0])
    own_rows = solve_rows(rows_in, *factor_parts)
    other_rows = swap_cores(own_rows)
    front = assemble(where, rows_in, after(entries, own_rows))
    factor, updated = update(where, own_rows, other_rows, columns, front, top)
    updated = updated.reshape(4, 1, BLK, 4, 1, BLK)
    return updated, factor.reshape(4, 1, BLK, P_SIZE)


def solution(mesh):
    in_specs = (
        P(None, "row", None, None, ("sub", "col"), None),
        P("sub", None, "row", None, None, "col", None),
        P(),
    )
    out_specs = (P(None, "row", None, None, ("sub", "col"), None), P(None, "row", None, None))
    return jax.shard_map(
        per_device, mesh=mesh, in_specs=in_specs, out_specs=out_specs, check_vma=False
    )
```

```python
import functools

import jax
import jax.numpy as jnp
from jax import lax
from jax.experimental import pallas as pl
from jax.experimental.pallas import tpu as pltpu
from jax.sharding import PartitionSpec as P

BLK = 128
FB = 64
UB = 48
P_SIZE = 1024
NPB = 8
GR = 16
NC = 8
CHIPS = GR * NC
F32 = jnp.float32
HIGHEST = lax.Precision.HIGHEST


def dot_full(a, b, dim_a, dim_b):
    return lax.dot_general(
        a, b, (((dim_a,), (dim_b,)), ((), ())), precision=HIGHEST, preferred_element_type=F32
    )


def split(x):
    high = x.astype(jnp.bfloat16)
    return high, (x - high.astype(F32)).astype(jnp.bfloat16)


def dot_split(a, b):
    def dot(x, y):
        return lax.dot_general(x, y, (((1,), (1,)), ((), ())), preferred_element_type=F32)

    return dot(a[0], b[0]) + (dot(a[0], b[1]) + dot(a[1], b[0]))


def split_rows(x):
    def head(y):
        return y.astype(jnp.bfloat16).astype(F32)

    high = head(x)
    mid = head(x - high)
    return high, mid, head(x - high - mid)


def stacked(parts):
    return jnp.concatenate(parts, 0).astype(jnp.bfloat16)


def reciprocal(x):
    guess = pltpu.reciprocal(x, approx=True)
    return guess * (2.0 - x * guess)


def row_of(x, t):
    return jnp.broadcast_to(x[t : t + 1, :], x.shape)


def col_of(x, t):
    return jnp.broadcast_to(x[:, t : t + 1], x.shape)


def products(columns, rows):
    parts = [c * r for c, r in zip(columns, rows, strict=True)]
    while len(parts) > 1:
        parts = [parts[2 * n] + parts[2 * n + 1] for n in range(len(parts) // 2)]
    return parts[0]


NEAR = 2


def factor_block(w):
    sub = lax.broadcasted_iota(jnp.int32, (8, BLK), 0)
    lane = lax.broadcasted_iota(jnp.int32, (8, BLK), 1)
    tiles = BLK // 8
    left = [w[8 * i : 8 * i + 8, :] for i in range(tiles)]
    right = [(lane == sub + 8 * i).astype(F32) for i in range(tiles)]
    uppers, inverses = [], []
    diag = [col_of(left[0], t) for t in range(8)]
    for s in range(tiles):
        rows, extra = left[s], right[s]
        raw, last = rows, s == tiles - 1
        ahead, later, near = [], [], {}
        if not last:
            ahead = [col_of(rows, 8 * s + 8 + t) for t in range(8)]
            later = [col_of(left[s + 1], 8 * s + 8 + t) for t in range(8)]
            near = {
                i: [col_of(left[i], 8 * s + t) for t in range(8)]
                for i in range(s + 1, min(tiles, s + 1 + NEAR))
            }
        u, v, pivots = rows, extra, None
        for t in range(0, 8, 2):
            c0, c1 = diag[t], diag[t + 1]
            a, b, d = row_of(c0, t), row_of(c1, t), row_of(c1, t + 1)
            inv_det = reciprocal(a * d - b * b)
            at0, at1 = sub == t, sub == t + 1
            either = at0 | at1
            g0 = jnp.where(at0, -d, jnp.where(at1, b, c0 * d - c1 * b))
            g1 = jnp.where(at0, b, jnp.where(at1, -a, c1 * a - c0 * b))
            h0, h1 = g0 * inv_det, g1 * inv_det
            ratio = b * reciprocal(a)
            u = jnp.where(at0, rows, jnp.where(at1, row_of(rows, t + 1) - ratio * row_of(rows, t), u))
            v = jnp.where(
                at0, extra, jnp.where(at1, row_of(extra, t + 1) - ratio * row_of(extra, t), v)
            )
            pivots = a if pivots is None else jnp.where(at0, a, pivots)
            pivots = jnp.where(at1, d - b * ratio, pivots)

            def reduce(x, soon=False):
                x0, x1, base = row_of(x, t), row_of(x, t + 1), jnp.where(either, 0.0, x)
                if soon:
                    return base - (g0 * x0 + g1 * x1) * inv_det
                return base - (h0 * x0 + h1 * x1)

            for c in range(t + 2, 8):
                diag[c] = reduce(diag[c], c < t + 4)
            ahead = [reduce(x) for x in ahead]
            rows, extra = reduce(rows), reduce(extra)
        scale = lax.rsqrt(pivots)
        uppers.append(jnp.where(lane >= sub + 8 * s, u * scale, 0.0))
        inverses.append(v * scale)
        if last:
            break
        diag = [
            later[c] - products(near[s + 1], [row_of(ahead[c], t) for t in range(8)])
            for c in range(8)
        ]
        row_terms = [row_of(rows, t) for t in range(8)]
        extra_terms = [row_of(extra, t) for t in range(8)]
        for i, columns in near.items():
            left[i] = left[i] - products(columns, row_terms)
            right[i] = right[i] - products(columns, extra_terms)
        if s + 1 + NEAR < tiles:
            high, mid, low = split_rows(raw)
            far_columns = stacked([high, high, mid, mid, high, low])
            high, mid, low = split_rows(jnp.concatenate([rows, extra], 1))
            far_rows = stacked([high, mid, high, mid, low, high])
            far = lax.dot_general(
                far_columns, far_rows, (((0,), (0,)), ((), ())), preferred_element_type=F32
            )
            for i in range(s + 1 + NEAR, tiles):
                left[i] = left[i] - far[8 * i : 8 * i + 8, :BLK]
                right[i] = right[i] - far[8 * i : 8 * i + 8, BLK:]
    return jnp.concatenate(uppers, 0), jnp.concatenate(inverses, 0)


WIDE = 2 * BLK
STRIP = 4 * BLK
STEPS = P_SIZE // WIDE
TRIANGLE = [(p, q) for q in range(NPB) for p in range(q, NPB)]
HALF = len(TRIANGLE) // 2


def cholesky_kernel(
    where_ref,
    own_ref,
    other_ref,
    low_hi,
    low_lo,
    inv_hi,
    inv_lo,
    top_ref,
    lower_ref,
    inverse_ref,
    panel,
    upper,
):
    first_core, grid_row = where_ref[0] == 0, where_ref[1]
    lower_ref[...] = jnp.zeros_like(lower_ref)

    def step(k, carry):
        for n in range(NPB):

            @pl.when(k == n)
            def _(n=n):
                start = n * BLK
                cols = slice(start, start + BLK)
                for p in range(n, NPB):
                    spot = TRIANGLE.index((p, n))
                    rows = slice(spot % HALF * 8, spot % HALF * 8 + 8)
                    own, other = own_ref[:, rows, :], other_ref[:, rows, :]
                    is_own = first_core if spot < HALF else jnp.logical_not(first_core)
                    block = jnp.swapaxes(jnp.where(is_own, own, other), 0, 1).reshape(BLK, BLK)
                    panel[(p - n) * BLK : (p - n + 1) * BLK, :] = block
                if n:
                    panel[: P_SIZE - start, :] -= dot_full(
                        lower_ref[start:, :start], lower_ref[cols, :start], 1, 1
                    )

        u, v = factor_block(panel[:BLK, :])
        upper[...] = u
        inverse_ref[k] = v
        for n in range(NPB):

            @pl.when(k == n)
            def _(n=n):
                start = n * BLK
                cols = slice(start, start + BLK)
                lower_ref[cols, cols] = upper[...].T
                if n < NPB - 1:
                    lower_ref[start + BLK :, cols] = dot_full(
                        panel[BLK : P_SIZE - start, :], inverse_ref[n], 1, 1
                    )

        return carry

    lax.fori_loop(0, NPB, step, 0)
    top_ref[...] = lower_ref[
        pl.ds(pl.multiple_of(jnp.minimum(grid_row, NPB - 1) * BLK, BLK), BLK), :
    ]
    low_hi[...], low_lo[...] = split(lower_ref[WIDE:, : P_SIZE - WIDE])
    for n in range(STEPS):
        a, b = inverse_ref[2 * n], inverse_ref[2 * n + 1]
        mid = lower_ref[(2 * n + 1) * BLK : (2 * n + 2) * BLK, 2 * n * BLK : (2 * n + 1) * BLK]
        corner = -dot_full(dot_full(b, mid, 1, 0), a, 1, 0)
        whole = jnp.concatenate(
            [
                jnp.concatenate([a, jnp.zeros((BLK, BLK), F32)], 1),
                jnp.concatenate([corner, b], 1),
            ],
            0,
        )
        inv_hi[n], inv_lo[n] = split(whole)


def cholesky(where, own, other):
    bf16 = jnp.bfloat16
    whole = pl.BlockSpec(memory_space=pltpu.VMEM)
    return pl.pallas_call(
        cholesky_kernel,
        in_specs=[pl.BlockSpec(memory_space=pltpu.SMEM), whole, whole],
        out_specs=[whole] * 5,
        out_shape=[jax.ShapeDtypeStruct((P_SIZE - WIDE, P_SIZE - WIDE), bf16)] * 2
        + [jax.ShapeDtypeStruct((STEPS, WIDE, WIDE), bf16)] * 2
        + [jax.ShapeDtypeStruct((BLK, P_SIZE), F32)],
        scratch_shapes=[
            pltpu.VMEM((P_SIZE, P_SIZE), F32),
            pltpu.VMEM((NPB, BLK, BLK), F32),
            pltpu.VMEM((P_SIZE, BLK), F32),
            pltpu.VMEM((BLK, BLK), F32),
        ],
        compiler_params=pltpu.CompilerParams(vmem_limit_bytes=60 * 2**20),
        cost_estimate=pl.CostEstimate(
            flops=1, bytes_accessed=1, transcendentals=0
        ),
        name="cholesky",
    )(where, own, other)


def solve_strip(strip, lower, inverse, done_hi, done_lo, factor=None, ready=None):
    for n in range(STEPS):
        cols, done = slice(n * WIDE, (n + 1) * WIDE), slice(0, n * WIDE)
        above = slice((n - 1) * WIDE, n * WIDE)
        part = strip[:, cols]
        if ready is not None:
            ready(n)
        if n:
            part = part - dot_split(
                (done_hi[:, done], done_lo[:, done]), (lower[0][above, done], lower[1][above, done])
            )
        part = dot_split(split(part), (inverse[0][n], inverse[1][n]))
        if factor is not None:
            factor[:, cols] = part
        done_hi[:, cols], done_lo[:, cols] = split(part)


def start_loads(strip_hbm, strip_ref, parts, sems):
    pairs = [(strip_hbm, strip_ref), *parts[2:]]
    for n in range(1, STEPS):
        spot = (slice((n - 1) * WIDE, n * WIDE), slice(0, n * WIDE))
        pairs += [(source.at[spot], target.at[spot]) for source, target in parts[:2]]
    loads = [pltpu.make_async_copy(a, b, sems.at[n]) for n, (a, b) in enumerate(pairs)]
    for load in loads:
        load.start()

    def ready(n):
        for load in loads[1 + 2 * n : 3 + 2 * n]:
            load.wait()

    return loads[0], ready


def column_kernel(
    col_hbm,
    low_hi_hbm,
    low_lo_hbm,
    inv_hi_hbm,
    inv_lo_hbm,
    col_hi,
    col_lo,
    col_ref,
    low_hi,
    low_lo,
    inv_hi,
    inv_lo,
    strip,
    sems,
):
    parts = ((low_hi_hbm, low_hi), (low_lo_hbm, low_lo), (inv_hi_hbm, inv_hi), (inv_lo_hbm, inv_lo))
    first, ready = start_loads(col_hbm, col_ref, parts, sems)
    first.wait()
    for b in range(4):
        part = jnp.swapaxes(col_ref[:, :, b * NPB : (b + 1) * NPB, :], 0, 1)
        part = jnp.swapaxes(part.reshape(BLK, NPB, BLK), 0, 1)
        for q in range(NPB):
            cols = slice(q * BLK, (q + 1) * BLK)
            strip[b * BLK : (b + 1) * BLK, cols] = part[q]
    solve_strip(strip, (low_hi, low_lo), (inv_hi, inv_lo), col_hi, col_lo, None, ready)


def solve_columns(col_strip, *factor_parts):
    inputs = (col_strip, *factor_parts)
    anywhere = pl.BlockSpec(memory_space=pl.ANY)
    return pl.pallas_call(
        column_kernel,
        in_specs=[anywhere] * len(inputs),
        out_specs=[pl.BlockSpec(memory_space=pltpu.VMEM)] * 2,
        out_shape=[jax.ShapeDtypeStruct((STRIP, P_SIZE), jnp.bfloat16)] * 2,
        scratch_shapes=[pltpu.VMEM(x.shape, x.dtype) for x in inputs]
        + [pltpu.VMEM((STRIP, P_SIZE), F32), pltpu.SemaphoreType.DMA((9,))],
        compiler_params=pltpu.CompilerParams(vmem_limit_bytes=60 * 2**20),
        cost_estimate=pl.CostEstimate(
            flops=200_000_000_000, bytes_accessed=9_000_000, transcendentals=0
        ),
        name="solve_columns",
    )(*inputs)


def row_kernel(
    own_hbm,
    low_hi_hbm,
    low_lo_hbm,
    inv_hi_hbm,
    inv_lo_hbm,
    factor_ref,
    own_ref,
    low_hi,
    low_lo,
    inv_hi,
    inv_lo,
    strip,
    row_hi,
    row_lo,
    sems,
):
    parts = ((low_hi_hbm, low_hi), (low_lo_hbm, low_lo), (inv_hi_hbm, inv_hi), (inv_lo_hbm, inv_lo))
    first, ready = start_loads(own_hbm.at[:, 16:, :], own_ref, parts, sems)
    first.wait()
    for h in range(2):
        part = jnp.swapaxes(own_ref[:, h * NPB : (h + 1) * NPB, :], 0, 1)
        for q in range(NPB):
            strip[h * BLK : (h + 1) * BLK, q * BLK : (q + 1) * BLK] = part[q]

    solve_strip(strip, (low_hi, low_lo), (inv_hi, inv_lo), row_hi, row_lo, factor_ref, ready)


def solve_rows(rows_in, *factor_parts):
    anywhere = pl.BlockSpec(memory_space=pl.ANY)
    half = (STRIP // 2, P_SIZE)
    return pl.pallas_call(
        row_kernel,
        in_specs=[anywhere] * 5,
        out_specs=pl.BlockSpec(memory_space=pltpu.VMEM),
        out_shape=jax.ShapeDtypeStruct(half, F32),
        scratch_shapes=[pltpu.VMEM((BLK, 16, BLK), F32)]
        + [pltpu.VMEM(x.shape, x.dtype) for x in factor_parts]
        + [pltpu.VMEM(half, F32)]
        + [pltpu.VMEM(half, jnp.bfloat16)] * 2
        + [pltpu.SemaphoreType.DMA((9,))],
        compiler_params=pltpu.CompilerParams(vmem_limit_bytes=60 * 2**20),
        cost_estimate=pl.CostEstimate(
            flops=2_000_000_000, bytes_accessed=5_000_000, transcendentals=0
        ),
        name="solve_rows",
    )(rows_in, *factor_parts)


def front_kernel(
    where_ref, sums_hbm, entry_hbm, front_hbm, sums_ref, entry_ref, front_ref, sems
):
    grid_row, grid_col = where_ref[1], where_ref[2]
    loads = [
        pltpu.make_async_copy(sums_hbm.at[:, :16, :], sums_ref, sems.at[0]),
        pltpu.make_async_copy(entry_hbm, entry_ref, sems.at[1]),
    ]
    for load in loads:
        load.start()
    for load in loads:
        load.wait()
    stores = []
    for b in range(4):
        if b % 2 == 0:
            blocks = jnp.swapaxes(sums_ref[:, b * 4 : b * 4 + 8, :], 0, 1)
        for d in range(4):
            sums = blocks[b % 2 * 4 + d]
            if b < d:
                sums = sums.T
            elif b == d:
                sums = jnp.where(grid_row >= grid_col, sums, sums.T)
            entry = entry_ref[pl.ds(b * STRIP + d, BLK, stride=4), :]
            front_ref[b * BLK : (b + 1) * BLK, d * BLK : (d + 1) * BLK] = entry + sums
        rows = slice(b * BLK, (b + 1) * BLK)
        stores.append(pltpu.make_async_copy(front_ref.at[rows], front_hbm.at[rows], sems.at[2 + b]))
        stores[-1].start()
    for store in stores:
        store.wait()


def assemble(where, rows_in, entries):
    anywhere = pl.BlockSpec(memory_space=pl.ANY)
    return pl.pallas_call(
        front_kernel,
        in_specs=[
            pl.BlockSpec(memory_space=pltpu.SMEM),
            anywhere,
            anywhere,
        ],
        out_specs=anywhere,
        out_shape=jax.ShapeDtypeStruct((STRIP, STRIP), F32),
        scratch_shapes=[
            pltpu.VMEM((BLK, 16, BLK), F32),
            pltpu.VMEM((4 * STRIP, BLK), F32),
            pltpu.VMEM((STRIP, STRIP), F32),
            pltpu.SemaphoreType.DMA((6,)),
        ],
        compiler_params=pltpu.CompilerParams(vmem_limit_bytes=60 * 2**20),
        cost_estimate=pl.CostEstimate(
            flops=1_000_000_000, bytes_accessed=4_000_000, transcendentals=0
        ),
        name="assemble",
    )(where, rows_in, entries)


def update_kernel(
    where_ref,
    own_hbm,
    other_hbm,
    col_hi_hbm,
    col_lo_hbm,
    front_hbm,
    top_hbm,
    factor_hbm,
    out_hbm,
    col_hi,
    col_lo,
    front_ref,
    top_ref,
    factor_ref,
    out_ref,
    product,
    sems,
):
    first_core, grid_row, grid_col = where_ref[0] == 0, where_ref[1], where_ref[2]
    pairs = [(col_hi_hbm, col_hi), (col_lo_hbm, col_lo), (front_hbm, front_ref), (top_hbm, top_ref)]
    loads = [pltpu.make_async_copy(a, b, sems.at[n]) for n, (a, b) in enumerate(pairs)]
    halves = factor_ref.at[: STRIP // 2], factor_ref.at[STRIP // 2 :]

    def load_rows(first, second):
        copies = [
            pltpu.make_async_copy(first, halves[0], sems.at[4]),
            pltpu.make_async_copy(second, halves[1], sems.at[5]),
        ]
        for copy in copies:
            copy.start()
        for load in loads:
            load.start()
        for copy in copies:
            copy.wait()

    @pl.when(first_core)
    def _():
        load_rows(own_hbm, other_hbm)

    @pl.when(jnp.logical_not(first_core))
    def _():
        load_rows(other_hbm, own_hbm)

    for load in loads:
        load.wait()

    @pl.when(grid_row < NPB)
    def _():
        factor_ref[:BLK, :] = top_ref[...]

    factor_store = pltpu.make_async_copy(factor_ref, factor_hbm, sems.at[6])
    factor_store.start()
    stores = [factor_store]
    product[...] = dot_split(split(factor_ref[...]), (col_hi[...], col_lo[...]))
    for b in range(4):
        for d in range(4):
            rows, cols = slice(b * BLK, (b + 1) * BLK), slice(d * BLK, (d + 1) * BLK)
            trail = product[rows, cols]
            if b == 0:
                trail = jnp.where(grid_row >= NPB, trail, 0.0)
            if d == 0:
                trail = jnp.where(grid_col >= NPB, trail, 0.0)
            out_ref[pl.ds(b * STRIP + d, BLK, stride=4), :] = front_ref[rows, cols] - trail
        spot = slice(b * STRIP, (b + 1) * STRIP)
        stores.append(pltpu.make_async_copy(out_ref.at[spot], out_hbm.at[spot], sems.at[7 + b]))
        stores[-1].start()
    for store in stores:
        store.wait()


def update(where, own, other, columns, front, top):
    inputs = (own, other, *columns, front, top)
    outputs = [
        jax.ShapeDtypeStruct((STRIP, P_SIZE), F32),
        jax.ShapeDtypeStruct((4 * STRIP, BLK), F32),
    ]
    anywhere = pl.BlockSpec(memory_space=pl.ANY)
    return pl.pallas_call(
        update_kernel,
        in_specs=[pl.BlockSpec(memory_space=pltpu.SMEM)] + [anywhere] * len(inputs),
        out_specs=[anywhere] * 2,
        out_shape=outputs,
        scratch_shapes=[pltpu.VMEM(x.shape, x.dtype) for x in (*inputs[2:], *outputs)]
        + [pltpu.VMEM((STRIP, STRIP), F32), pltpu.SemaphoreType.DMA((11,))],
        compiler_params=pltpu.CompilerParams(vmem_limit_bytes=60 * 2**20),
        cost_estimate=pl.CostEstimate(
            flops=2_000_000_000, bytes_accessed=9_000_000, transcendentals=0
        ),
        name="update",
    )(where, *inputs)


def split_kernel(counts, child_ref, entry_ref, out_ref):
    sources = [(child_ref, 6 * BLK * b + d, 6) for b, n in enumerate(counts) for d in range(n)]
    sources += [(entry_ref, STRIP * b, 4) for b in range(4)]
    for slot, (ref, start, stride) in enumerate(sources):
        out_ref[pl.ds(slot, BLK, stride=16), :] = ref[pl.ds(start, BLK, stride=stride), :]


def split_blocks(counts, child, entries):
    whole = pl.BlockSpec(memory_space=pltpu.VMEM)
    return pl.pallas_call(
        functools.partial(split_kernel, counts),
        in_specs=[whole] * 2,
        out_specs=whole,
        out_shape=jax.ShapeDtypeStruct((BLK * 16, BLK), F32),
        compiler_params=pltpu.CompilerParams(vmem_limit_bytes=60 * 2**20),
        cost_estimate=pl.CostEstimate(flops=0, bytes_accessed=3_000_000, transcendentals=0),
        name="split_blocks",
    )(child, entries)


def pack_kernel(inverse_map_ref, own_ref, other_ref, panel_ref, out_ref):
    for p in range(FB):
        b, r = divmod(p, GR)
        total = jnp.zeros((4 * NC, BLK), F32)
        for k, child in enumerate((own_ref, other_ref)):
            spot = inverse_map_ref[k, p]
            total = total + jnp.where(spot >= 0, child[jnp.maximum(spot, 0)], 0.0)
        for d in range(4):
            out_ref[pl.ds(r * 32 + b * 4 + d, NC, stride=GR * 32), :] = total[d * NC : (d + 1) * NC]
    for h in range(2):
        for r in range(GR):
            rows = panel_ref[h, r]
            for c in range(NC):
                out_ref[pl.ds((c * GR + r) * 32 + 16 + h * 8, NPB), :] = rows


def pack(inverse_maps, own, other, panel):
    whole = pl.BlockSpec(memory_space=pltpu.VMEM)
    return pl.pallas_call(
        pack_kernel,
        in_specs=[pl.BlockSpec(memory_space=pltpu.SMEM)] + [whole] * 3,
        out_specs=whole,
        out_shape=jax.ShapeDtypeStruct((CHIPS * 32, BLK), F32),
        compiler_params=pltpu.CompilerParams(vmem_limit_bytes=12 * 2**20),
        cost_estimate=pl.CostEstimate(flops=0, bytes_accessed=8_000_000, transcendentals=0),
        name="pack",
    )(inverse_maps, own, other, panel)


def to_chips(x):
    return lax.all_to_all(x, ("col", "row"), 0, 0)


def after(x, earlier):
    return lax.optimization_barrier((x, earlier))[0]


def swap_cores(x):
    return lax.ppermute(x, "sub", [(0, 1), (1, 0)])


def per_device(front_entries, child_updates, row_maps):
    my_row = lax.axis_index("row")
    my_col = lax.axis_index("col")
    my_sub = lax.axis_index("sub")
    entries = front_entries[:, 0, :, :, 0, :]
    child_own = child_updates[0, :, 0, :, :, 0, :]
    own_map = lax.dynamic_index_in_dim(row_maps, my_sub, 0, keepdims=False)
    other_map = lax.dynamic_index_in_dim(row_maps, 1 - my_sub, 0, keepdims=False)
    blocks = jnp.arange(FB, dtype=jnp.int32)
    where = jnp.stack([my_sub, my_row, my_sub * NC + my_col]).astype(jnp.int32)

    counts = [2 * b + 2 for b in range(3)]
    entries = entries.reshape(4 * STRIP, BLK)
    slices_out = split_blocks(counts, child_own.reshape(18 * BLK, BLK), entries)
    slices_out = slices_out.reshape(CHIPS, 16, BLK)
    slices_in = to_chips(slices_out).reshape(NC, GR, 16, BLK)
    lower_child, start = [], 0
    for count in counts:
        part = slices_in[:, :, start : start + count].transpose(1, 2, 0, 3)
        part = jnp.pad(part, ((0, 0), (0, 6 - count), (0, 0), (0, 0)))
        lower_child.append(part.reshape(GR, UB, BLK))
        start += count
    lower_child = jnp.concatenate(lower_child, 0)
    entry_rows = slices_in[:, :, start:].transpose(2, 1, 0, 3).reshape(FB, NPB, BLK)

    row_pick = (own_map[None, :] == blocks[:, None]).astype(F32)
    col_pick = (own_map[None, :NPB] == blocks[:NPB, None]).astype(F32)
    both_pick = (row_pick[:, None, :, None] * col_pick[None, :, None, :]).reshape(
        FB * NPB, UB * NPB
    )
    child_panel = lower_child[:, :NPB].reshape(UB * NPB, BLK)
    placed = dot_full(both_pick, child_panel, 1, 0).reshape(FB, NPB, BLK)
    placed = placed + jnp.where(my_sub == 0, entry_rows, 0.0)
    panel_rows = placed + swap_cores(placed)

    by_grid = panel_rows.reshape(4, 2, NC, NPB, BLK)
    for_cols = lax.dynamic_index_in_dim(by_grid, my_sub, 1, keepdims=False).transpose(1, 0, 2, 3)
    triangle = jnp.concatenate([panel_rows[q:NPB, q] for q in range(NPB)], 0)
    triangle = lax.dynamic_index_in_dim(triangle.reshape(2, HALF, BLK), my_sub, 0, False)
    triangle = jnp.broadcast_to(triangle[None], (NC, HALF, BLK))
    along_col = lax.all_to_all(
        jnp.concatenate([for_cols.reshape(NC, 32, BLK), triangle], 1), "col", 0, 0
    )
    col_part = along_col[:, :32]
    lead = along_col[:, 32:].transpose(1, 0, 2).reshape(HALF * 8, BLK)
    lead = after(lead, col_part)
    lead = lax.all_to_all(jnp.broadcast_to(lead[None], (GR, HALF * 8, BLK)), "row", 0, 0)

    ids = jnp.arange(UB, dtype=jnp.int32)
    below = (ids[:, None] > ids[None, :])[:, :, None]
    on_or_below = (ids[:, None] >= ids[None, :])[:, :, None]
    lower_child = after(lower_child, along_col)
    child = jnp.where(on_or_below, lower_child, 0.0)
    child = child + jnp.where(below, lower_child, 0.0).transpose(1, 0, 2)
    col_ids = blocks.reshape(4, 2, NC)
    own_cols = lax.dynamic_index_in_dim(col_ids, my_sub, 1, keepdims=False).reshape(-1)
    other_cols = lax.dynamic_index_in_dim(col_ids, 1 - my_sub, 1, keepdims=False).reshape(-1)
    all_cols = jnp.concatenate([own_cols, other_cols])
    widen = (own_map[None, :] == all_cols[:, None]).astype(F32)
    widened = jnp.einsum("qj,ijl->iql", widen, child, precision=HIGHEST)
    kept, arrived = widened[:, : FB // 2], swap_cores(widened[:, FB // 2 :])

    both_maps = jnp.stack([own_map, other_map])
    hit = both_maps[:, None, :] == blocks[None, :, None]
    inverse_maps = jnp.max(jnp.where(hit, ids, -1), axis=2)
    halves = panel_rows.reshape(2, 2, GR, NPB, BLK)
    for_rows = lax.dynamic_index_in_dim(halves, my_sub, 0, keepdims=False)
    rows_out = pack(inverse_maps, kept, arrived, for_rows).reshape(CHIPS, 32, BLK)
    lead, rows_out = lax.optimization_barrier((lead, rows_out))
    other_lead = swap_cores(lead)
    col_strip = lax.all_gather(after(col_part, lead), "row", axis=0)
    rows_in = to_chips(rows_out)

    *factor_parts, top = cholesky(where, lead, other_lead)
    columns = solve_columns(col_strip, *factor_parts)
    rows_in = after(rows_in, columns[0])
    own_rows = solve_rows(rows_in, *factor_parts)
    other_rows = swap_cores(own_rows)
    front = assemble(where, rows_in, after(entries, own_rows))
    factor, updated = update(where, own_rows, other_rows, columns, front, top)
    updated = updated.reshape(4, 1, BLK, 4, 1, BLK)
    return updated, factor.reshape(4, 1, BLK, P_SIZE)


def solution(mesh):
    in_specs = (
        P(None, "row", None, None, ("sub", "col"), None),
        P("sub", None, "row", None, None, "col", None),
        P(),
    )
    out_specs = (P(None, "row", None, None, ("sub", "col"), None), P(None, "row", None, None))
    return jax.shard_map(
        per_device, mesh=mesh, in_specs=in_specs, out_specs=out_specs, check_vma=False
    )
```
